32 devices in a mesh: mass: 4 (over y, x), shard: 8 (over z, core).
Axes of the slice: x: 2, y: 2, z: 4, core: 2. Of those that a mesh axis runs over, the one named last changes fastest.
Arguments:
- queries: bfloat16 [512, 8192], P(('mass', 'shard')), may hold values from -6 to 6
- library: bfloat16 [32768, 8192], P(('mass', 'shard')), may hold values from -0.0625 to 0.0625
- routes: int32 [512, 1], P(('mass', 'shard')), may hold values from 0 to 3; in each aligned block of 16 rows (0 to 15, 16 to 31, ...) at most 8 rows name the same one
- offsets: int32 [512], P(('mass', 'shard')), may hold values from -2048 to 2048
Outputs:
- best_scores: float32 [512, 16], P(('mass', 'shard'))
The draws below stay inside these ranges and needn't reach their ends.
Inputs may be any that keep to these rules, and one draw needn't show every extreme that they name: `routes`: in each device's aligned block of 16 queries at most 8 go to one mass group, and some group gets exactly 8 from some device.
All inputs are finite; a program needn't handle non-finite values.
Results may differ from the reference program's by a relative error of at most 0.00087.
Values may be sent and summed in bfloat16 or wider, within the bound.
A program may use at most 128 MiB of HBM per device.

```python
import math
import jax
import jax.numpy as jnp
import numpy as np
from jax import lax

BINS = 8192
MAX_SHIFT = 2048
TOP_K = 16
LIB_DEV = 1024
Q_DEV = 16
CAP = 8
Q_TOTAL = 512
LIB = 32768
N_MASS = 4
N_SHARD = 8
DEVICES = 32


def touch_ends(result, stream_key, smallest, top_value):
    index_at = [jax.random.randint(jax.random.fold_in(stream_key, axis), (), 0, length) for axis, length in enumerate(result.shape)]
    widest = result.shape.index(max(result.shape))
    beside = index_at[:widest] + [(index_at[widest] + 1) % result.shape[widest]] + index_at[widest + 1:]
    return result.at[tuple(index_at)].set(smallest).at[tuple(beside)].set(top_value)


def shard_levels(rng, extent, split, least, largest):
    factor_of, own = 1.0, jax.random.fold_in(rng, 6)
    for position, blocks in split:
        steps = jnp.exp(jax.random.uniform(jax.random.fold_in(own, position), (blocks,), jnp.float32, least / len(split), largest / len(split)))
        factor_of = factor_of * jnp.repeat(steps, extent[position] // blocks).reshape([-1 if axis == position else 1 for axis in range(len(extent))])
    return factor_of


def shared_out(rng, own, number, rows, count, top, bound, lean):
    order = jax.random.permutation(rng, count)
    crowded, common = shares(count, rows * top, bound, lean, True), shares(count, rows * top, bound, lean, False)
    places = jnp.arange(count)

    def named(sizes, rotation):
        used = int((sizes > 0).sum())
        fixed = max(1, used // 4)
        moved = fixed + (places - fixed + rotation * (used - fixed)) % max(1, count - fixed)
        return jnp.zeros((count,), jnp.int32).at[order[jnp.where(places < fixed, places, moved)]].set(jnp.asarray(sizes, jnp.int32))

    sizes = jnp.where(number % 4 == 0, named(crowded, number // 4), named(common, number - number // 4 - 1))
    mixed = jax.random.permutation(jax.random.fold_in(own, 3), count)
    giver, taker = mixed[0:count // 2 * 2:2], mixed[1:count // 2 * 2:2]
    margin = jnp.minimum(sizes[giver] - 1, bound - sizes[taker]) // 2
    margin = jnp.where((giver == order[0]) | (taker == order[0]) | (sizes[taker] == 0), 0, jnp.maximum(margin, 0))
    moved = jax.random.randint(jax.random.fold_in(own, 4), (count // 2,), 0, 1 << 20) % (margin + 1)
    sizes = sizes.at[giver].add(-moved).at[taker].add(moved)
    labels = jnp.searchsorted(jnp.cumsum(sizes), jnp.arange(rows * top), side="right").astype(jnp.int32)
    listing = labels.reshape(top, rows).T
    listing = listing[jax.random.permutation(jax.random.fold_in(own, 1), rows)]
    rotation = jax.random.randint(jax.random.fold_in(own, 2), (rows, 1), 0, top)
    return jnp.take_along_axis(listing, (jnp.arange(top)[None, :] + rotation) % top, axis=1)


def shares(number_of, total, reach, skew, full):
    weights = [(1 << 20) // math.isqrt(standing ** skew) + 1 for standing in range(1, number_of + 1)]
    largest = reach if full else min(reach, max(-(-total // number_of), total * weights[0] // sum(weights)))
    least = 1 if total - largest >= number_of - 1 else 0
    counts, spare = [largest] + [least] * (number_of - 1), total - largest - least * (number_of - 1)
    while spare > 0:
        movable = [i for i in range(1, number_of) if counts[i] < largest] or [i for i in range(1, number_of) if counts[i] < reach]
        mass, remaining = sum([weights[i] for i in movable]), spare
        for i in movable:
            extra = min(reach - counts[i], max(1, remaining * weights[i] // mass), spare)
            counts[i] = counts[i] + extra
            spare = spare - extra
    return np.array(counts)


def centred(rng, dims, spread, bound, shards=(), kind=jnp.bfloat16):
    entries = spread * jax.random.normal(rng, dims, jnp.float32)
    if shards:
        entries = entries * shard_levels(rng, dims, shards, -0.22, 0.18)
    return jnp.clip(entries, -bound, bound).astype(kind)


def setup_inputs(seed: int = 0) -> dict:
    keys = jax.random.split(jax.random.key(seed), 5)
    queries = centred(keys[0], (Q_TOTAL, BINS), 1.0, 6.0, ((0, 32),))
    library = centred(keys[1], (LIB, BINS), BINS ** -0.5, 0.0625, ((0, 32),))
    routes_keys = jax.random.split(jax.random.fold_in(keys[2], 1), Q_TOTAL // Q_DEV)
    routes_turns = jax.random.permutation(jax.random.fold_in(keys[2], 3), Q_TOTAL // Q_DEV)
    routes = jax.vmap(lambda own, number: shared_out(jax.random.fold_in(keys[2], 2), own, number, Q_DEV, N_MASS, 1, CAP, 2))(routes_keys, routes_turns).reshape((Q_TOTAL, 1))
    offsets = touch_ends(jax.random.randint(keys[3], (Q_TOTAL,), -MAX_SHIFT, MAX_SHIFT + 1), jax.random.fold_in(keys[3], 1), -MAX_SHIFT, MAX_SHIFT).astype(jnp.int32)
    return dict(queries=queries, library=library, routes=routes, offsets=offsets)


def shifted_spectra(queries, offsets):
    bin_count = queries.shape[1]
    positions = jnp.arange(bin_count, dtype=jnp.int32)
    source_bin = positions[None, :] - offsets[:, None].astype(jnp.int32)
    inside = (source_bin >= 0) & (source_bin < bin_count)
    shifted = jnp.take_along_axis(queries, jnp.clip(source_bin, 0, bin_count - 1), axis=1)
    combined = queries.astype(jnp.float32) + jnp.where(inside, shifted.astype(jnp.float32), jnp.float32(0.0))
    scale_factor = lax.rsqrt(lax.optimization_barrier(jnp.mean(combined * combined, axis=1, keepdims=True)) + 1e-06)
    return (combined * scale_factor).astype(jnp.bfloat16)

def block_ranks(dest_group):
    length = dest_group.shape[0]
    position_ids = jnp.arange(length, dtype=jnp.int32)
    earlier = (dest_group[:, None] == dest_group[None, :]) & (position_ids[:, None] > position_ids[None, :])
    return lax.optimization_barrier(jnp.sum(earlier.astype(jnp.int32), axis=1)).astype(jnp.int32)

def reference(queries, library, routes, offsets):
    spectra = shifted_spectra(queries, offsets)
    dest_group = routes[:, 0].astype(jnp.int32)
    ranks_all = jax.vmap(block_ranks)(dest_group.reshape(DEVICES, Q_DEV)).reshape(-1)
    query_ids = jnp.arange(DEVICES * Q_DEV, dtype=jnp.int32)
    slot_index = query_ids // Q_DEV * CAP + ranks_all
    slot_total = DEVICES * CAP
    grouped_library = library.reshape(N_MASS, N_SHARD * LIB_DEV, BINS)

    def per_group(operands):
        library_group, group_id = operands
        target = jnp.where(dest_group == group_id, slot_index, slot_total).astype(jnp.int32)
        picker = jnp.zeros((slot_total + 1,), jnp.int32).at[target].set(query_ids)
        filled = jnp.zeros((slot_total + 1,), jnp.int32).at[target].set(1)
        picked = jnp.take(spectra, picker[:slot_total], axis=0)
        picked = jnp.where(filled[:slot_total, None] == 1, picked, jnp.zeros_like(picked))
        scores = lax.dot_general(picked, library_group, (((1,), (1,)), ((), ())), preferred_element_type=jnp.float32)
        return lax.top_k(scores, TOP_K)[0]
    results = lax.map(per_group, (grouped_library, jnp.arange(N_MASS, dtype=jnp.int32)))
    return results[dest_group, slot_index]
```

```python
import functools

import jax
import jax.numpy as jnp
from jax import lax
from jax.experimental import pallas as pl
from jax.experimental.pallas import tpu as pltpu
from jax.sharding import PartitionSpec as P

MESH = pl.DeviceIdType.MESH
MAX_SHIFT = 2048
TOP_K = 16
LANES = 128
F32 = jnp.float32
BF16 = jnp.bfloat16


def comparators(count):
    pairs = []
    p = 1
    while p < count:
        k = p
        while k >= 1:
            for j in range(k % p, count - k, 2 * k):
                for i in range(min(k, count - j - k)):
                    if (i + j) // (2 * p) == (i + j + k) // (2 * p):
                        pairs.append((i + j, i + j + k))
            k //= 2
        p *= 2
    return pairs


def exchange(values, pairs):
    values = list(values)
    for i, j in pairs:
        a, b = values[i], values[j]
        values[i], values[j] = jnp.maximum(a, b), jnp.minimum(a, b)
    return values


SORT = comparators(TOP_K)
BITONIC = [
    (i, i + d) for d in (8, 4, 2, 1) for i in range(TOP_K) if i & d == 0
]


def merge(first, second):
    kept = [jnp.maximum(first[i], second[TOP_K - 1 - i]) for i in range(TOP_K)]
    return exchange(kept, BITONIC)


def spectra_kernel(mass_count, queries_ref, offsets_ref, routes_ref, routes_row_ref, halves_ref, own_ref):
    rows, bins = queries_ref.shape
    half = bins // 2
    capacity = rows // 2
    core = lax.rem(lax.axis_index("shard"), 2)
    plain = queries_ref[...].astype(F32)
    margin = jnp.zeros((rows, MAX_SHIFT), F32)
    current = jnp.concatenate([margin, plain, margin], axis=1)
    start = MAX_SHIFT - offsets_ref[...]
    step = 2 * MAX_SHIFT
    current = jnp.where(
        (start & step) != 0,
        jnp.concatenate([current[:, step:], jnp.zeros((rows, step), F32)], axis=1),
        current,
    )
    step //= 2
    while step >= LANES:
        width = bins + step
        current = jnp.where(
            (start & step) != 0, current[:, step : step + width], current[:, :width]
        )
        step //= 2
    width = bins + LANES
    while step >= 1:
        moved = pltpu.roll(current, width - step, 1)
        current = jnp.where((start & step) != 0, moved, current)
        step //= 2
    combined = plain + current[:, :bins]
    scale = lax.rsqrt(jnp.sum(combined * combined, axis=1, keepdims=True) * (1.0 / bins) + 1e-06)
    spectra = (combined * scale).astype(BF16)
    group = routes_ref[...]
    before = lax.broadcasted_iota(jnp.int32, (rows, rows), 0) > lax.broadcasted_iota(
        jnp.int32, (rows, rows), 1
    )
    earlier = (group == routes_row_ref[...]) & before
    rank = jnp.sum(jnp.where(earlier, 1.0, 0.0), axis=1, keepdims=True).astype(jnp.int32)
    lane = lax.broadcasted_iota(jnp.int32, (rows, LANES), 1)
    slot = group * (2 * capacity) + core * capacity + rank
    hot = jnp.where(lane == slot, 1.0, 0.0).astype(BF16)
    own_ref[...] = jnp.where(lane == group * capacity + rank, 1.0, 0.0)
    for part in range(2):
        halves_ref[part, :, :half] = spectra[:, part * half : (part + 1) * half]
        halves_ref[part, :, half:] = hot


def search_kernel(
    mass_count,
    shard_count,
    halves_ref,
    own_ref,
    library_ref,
    out_ref,
    lib,
    held,
    packed,
    slots,
    scores,
    outgoing,
    lists,
    lib_sem,
    start_sem,
    line_send,
    line_recv,
    layer_send,
    layer_recv,
    local_sem,
    pair_send,
    pair_recv,
    list_send,
    list_recv,
):
    places = shard_count // 2
    rows = halves_ref.shape[1]
    half = halves_ref.shape[2] - LANES
    cap = rows // 2
    block = mass_count * rows
    total = places * block
    mass = lax.axis_index("mass")
    shard = lax.axis_index("shard")
    place = shard // 2
    core = lax.rem(shard, 2)
    sibling = (mass, shard + 1 - 2 * core)
    device_count = mass_count * shard_count
    me = mass * shard_count + shard

    lib_copy = pltpu.make_async_copy(library_ref, lib, lib_sem)
    lib_copy.start()
    barrier = pltpu.get_barrier_semaphore()

    def greet(k, carry):
        other = lax.rem(me + k, device_count)
        pl.semaphore_signal(
            barrier,
            inc=1,
            device_id=(other // shard_count, lax.rem(other, shard_count)),
            device_id_type=MESH,
        )
        return carry

    lax.fori_loop(1, device_count, greet, 0)
    pl.semaphore_wait(barrier, device_count - 1)

    mine = pl.ds(pl.multiple_of(core * rows, rows), rows)
    swap = pltpu.make_async_remote_copy(
        src_ref=halves_ref.at[1 - core],
        dst_ref=held.at[place, mine],
        send_sem=start_sem.at[0],
        recv_sem=start_sem.at[1],
        device_id=sibling,
        device_id_type=MESH,
    )
    swap.start()
    keep = pltpu.make_async_copy(halves_ref.at[core], held.at[place, mine], start_sem.at[2])
    keep.start()
    keep.wait()
    swap.wait_recv()

    def line_copy(origin, way):
        return pltpu.make_async_remote_copy(
            src_ref=held.at[origin],
            dst_ref=held.at[origin],
            send_sem=line_send.at[way, origin],
            recv_sem=line_recv.at[origin],
            device_id=(mass, shard + (2 if way == 0 else -2)),
            device_id_type=MESH,
        )

    def layer_copy(origin, hop):
        target = lax.rem(mass + hop, mass_count)
        return pltpu.make_async_remote_copy(
            src_ref=packed.at[origin, pl.ds(pl.multiple_of(target * rows, rows), rows)],
            dst_ref=slots.at[
                core, pl.ds(pl.multiple_of(origin * block + mass * rows, rows), rows)
            ],
            send_sem=layer_send.at[origin, hop],
            recv_sem=layer_recv.at[origin, hop],
            device_id=(target, shard),
            device_id_type=MESH,
        )

    def layer_arrival(origin, hop):
        source = lax.rem(mass + mass_count - hop, mass_count)
        return pltpu.make_async_remote_copy(
            src_ref=packed.at[origin, pl.ds(0, rows)],
            dst_ref=slots.at[
                core, pl.ds(pl.multiple_of(origin * block + source * rows, rows), rows)
            ],
            send_sem=layer_send.at[origin, hop],
            recv_sem=layer_recv.at[origin, hop],
            device_id=(source, shard),
            device_id_type=MESH,
        )

    def local_copy(origin):
        return pltpu.make_async_copy(
            packed.at[origin, pl.ds(pl.multiple_of(mass * rows, rows), rows)],
            slots.at[core, pl.ds(pl.multiple_of(origin * block + mass * rows, rows), rows)],
            local_sem.at[origin],
        )

    def pair_copy(origin, part):
        span = slots.at[part, pl.ds(pl.multiple_of(origin * block, block), block)]
        return pltpu.make_async_remote_copy(
            src_ref=span,
            dst_ref=span,
            send_sem=pair_send.at[origin],
            recv_sem=pair_recv.at[origin],
            device_id=sibling,
            device_id_type=MESH,
        )

    def dispatch(origin):
        hot = held[origin, :, half:].astype(F32).T[:block].astype(BF16)
        tile = 512

        def pack(j, carry):
            span = pl.ds(pl.multiple_of(j * tile, tile), tile)
            packed[origin, :, span] = jnp.dot(
                hot, held[origin, :, span], preferred_element_type=F32
            ).astype(BF16)
            return carry

        lax.fori_loop(0, half // tile, pack, 0)
        for hop in range(1, mass_count):
            layer_copy(origin, hop).start()
        local_copy(origin).start()

    def hand_over(origin):
        local_copy(origin).wait()
        for hop in range(1, mass_count):
            layer_arrival(origin, hop).wait_recv()
        pair_copy(origin, core).start()

    @pl.when(place + 1 < places)
    def _():
        line_copy(place, 0).start()

    @pl.when(place > 0)
    def _():
        line_copy(place, 1).start()

    dispatch(place)

    def advance(t, carry):
        below, above = place - 1 - t, place + 1 + t

        @pl.when(below >= 0)
        def _():
            line_copy(below, 0).wait_recv()

            @pl.when(place + 1 < places)
            def _():
                line_copy(below, 0).start()

            dispatch(below)

        @pl.when(above < places)
        def _():
            line_copy(above, 1).wait_recv()

            @pl.when(place > 0)
            def _():
                line_copy(above, 1).start()

            dispatch(above)

        @pl.when(below + 1 >= 0)
        def _():
            hand_over(below + 1)

        @pl.when((above - 1 < places) & (t > 0))
        def _():
            hand_over(above - 1)

        return carry

    lax.fori_loop(0, places - 1, advance, 0)
    for last in (place - (places - 1), place + (places - 1)):

        @pl.when((last >= 0) & (last < places))
        def _():
            hand_over(last)

    lax.fori_loop(
        0, places, lambda o, x: (pair_copy(o, 1 - core).wait_recv(), x)[1], 0
    )
    lib_copy.wait()

    lib_rows = lib.shape[0]
    tall, wide = min(512, lib_rows), min(256, total)

    def score(k, carry):
        i, j = k // (total // wide), lax.rem(k, total // wide)
        down = pl.ds(pl.multiple_of(i * tall, tall), tall)
        across = pl.ds(pl.multiple_of(j * wide, wide), wide)
        sums = None
        for part in range(2):
            term = lax.dot_general(
                lib[down, part * half : (part + 1) * half],
                slots[part, across, :],
                (((1,), (1,)), ((), ())),
                preferred_element_type=F32,
            )
            sums = term if sums is None else sums + term
        scores[down, across] = sums
        return carry

    lax.fori_loop(0, (lib_rows // tall) * (total // wide), score, 0)

    sub = lax.broadcasted_iota(jnp.int32, (8, LANES), 0)

    def as_columns(values):
        upper, lower = values[0], values[8]
        for i in range(1, 8):
            upper = jnp.where(sub == i, values[i], upper)
            lower = jnp.where(sub == i, values[8 + i], lower)
        rest = jnp.zeros((LANES - TOP_K, LANES), F32)
        return jnp.concatenate([upper, lower, rest], axis=0).T

    stride = lib_rows // TOP_K

    def best(tile, carry):
        across = pl.ds(pl.multiple_of(tile * LANES, LANES), LANES)

        def more(r, kept):
            fresh = [
                scores[pl.ds(pl.multiple_of(i * stride + r * 8, 8), 8), across]
                for i in range(TOP_K)
            ]
            return tuple(merge(kept, exchange(fresh, SORT)))

        kept = tuple(jnp.full((8, LANES), -jnp.inf, F32) for _ in range(TOP_K))
        kept = lax.fori_loop(0, stride // 8, more, kept)
        for d in (4, 2, 1):
            kept = merge(kept, [pltpu.roll(x, d, 0) for x in kept])
        outgoing[across, :] = as_columns(kept)
        return carry

    lax.fori_loop(0, total // LANES, best, 0)

    def list_copy(k):
        other = lax.rem(me + k, device_count)
        to_mass, to_shard = other // shard_count, lax.rem(other, shard_count)
        at = ((to_shard // 2) * mass_count + to_mass) * 2 + lax.rem(to_shard, 2)
        return pltpu.make_async_remote_copy(
            src_ref=outgoing.at[pl.ds(pl.multiple_of(at * cap, cap), cap)],
            dst_ref=lists.at[
                pl.ds(pl.multiple_of((shard * mass_count + mass) * cap, cap), cap)
            ],
            send_sem=list_send.at[k],
            recv_sem=list_recv.at[k],
            device_id=(to_mass, to_shard),
            device_id_type=MESH,
        )

    def list_arrival(k):
        other = lax.rem(me + device_count - k, device_count)
        from_mass, from_shard = other // shard_count, lax.rem(other, shard_count)
        return pltpu.make_async_remote_copy(
            src_ref=outgoing.at[pl.ds(0, cap)],
            dst_ref=lists.at[
                pl.ds(pl.multiple_of((from_shard * mass_count + from_mass) * cap, cap), cap)
            ],
            send_sem=list_send.at[k],
            recv_sem=list_recv.at[k],
            device_id=(from_mass, from_shard),
            device_id_type=MESH,
        )

    lax.fori_loop(1, device_count, lambda k, x: (list_copy(k).start(), x)[1], 0)
    own_at = ((place * mass_count + mass) * 2 + core) * cap
    lists[pl.ds(pl.multiple_of((shard * mass_count + mass) * cap, cap), cap), :] = outgoing[
        pl.ds(pl.multiple_of(own_at, cap), cap), :
    ]
    lax.fori_loop(1, device_count, lambda k, x: (list_arrival(k).wait_recv(), x)[1], 0)

    kept = None
    for tile in range(device_count * cap // LANES):
        turned = lists[tile * LANES : (tile + 1) * LANES, :].T
        fresh = [jnp.broadcast_to(turned[i : i + 1, :], (8, LANES)) for i in range(TOP_K)]
        kept = fresh if kept is None else merge(kept, fresh)
    turn = mass_count * cap
    while turn < LANES:
        kept = merge(kept, [pltpu.roll(x, turn, 1) for x in kept])
        turn *= 2
    chosen = jnp.dot(
        own_ref[...],
        as_columns(kept),
        preferred_element_type=F32,
        precision=lax.Precision.HIGHEST,
    )
    out_ref[...] = chosen[:, :TOP_K]

    swap.wait_send()

    def finish(origin, carry):
        @pl.when((place + 1 < places) & (origin <= place))
        def _():
            line_copy(origin, 0).wait_send()

        @pl.when((place > 0) & (origin >= place))
        def _():
            line_copy(origin, 1).wait_send()

        for hop in range(1, mass_count):
            layer_copy(origin, hop).wait_send()
        pair_copy(origin, core).wait_send()
        return carry

    lax.fori_loop(0, places, finish, 0)
    lax.fori_loop(1, device_count, lambda k, x: (list_copy(k).wait_send(), x)[1], 0)


def per_device(mass_count, shard_count, queries, library, routes, offsets):
    rows, bins = queries.shape
    half = bins // 2
    places = shard_count // 2
    cap = rows // 2
    block = mass_count * rows
    total = places * block
    device_count = mass_count * shard_count
    vmem = pl.BlockSpec(memory_space=pltpu.VMEM)
    halves, own = pl.pallas_call(
        functools.partial(spectra_kernel, mass_count),
        out_shape=(
            jax.ShapeDtypeStruct((2, rows, half + LANES), BF16),
            jax.ShapeDtypeStruct((rows, LANES), F32),
        ),
        in_specs=[vmem] * 4,
        out_specs=(vmem, vmem),
        compiler_params=pltpu.CompilerParams(vmem_limit_bytes=32 * 2**20),
    )(queries, offsets[:, None], routes, routes.reshape(1, rows))
    dma = pltpu.SemaphoreType.DMA
    return pl.pallas_call(
        functools.partial(search_kernel, mass_count, shard_count),
        out_shape=jax.ShapeDtypeStruct((rows, TOP_K), F32),
        in_specs=[vmem, vmem, pl.BlockSpec(memory_space=pl.ANY)],
        out_specs=vmem,
        scratch_shapes=[
            pltpu.VMEM(library.shape, BF16),
            pltpu.VMEM((places, 2 * rows, half + LANES), BF16),
            pltpu.VMEM((places, block, half), BF16),
            pltpu.VMEM((2, total, half), BF16),
            pltpu.VMEM((library.shape[0], total), F32),
            pltpu.VMEM((total, LANES), F32),
            pltpu.VMEM((device_count * cap, LANES), F32),
            dma,
            dma((3,)),
            dma((2, places)),
            dma((places,)),
            dma((places, mass_count)),
            dma((places, mass_count)),
            dma((places,)),
            dma((places,)),
            dma((places,)),
            dma((device_count,)),
            dma((device_count,)),
        ],
        compiler_params=pltpu.CompilerParams(
            collective_id=0, has_side_effects=True, vmem_limit_bytes=56 * 2**20
        ),
    )(halves, own, library)


def solution(mesh):
    placed = (
        P(("mass", "shard"), None),
        P(("mass", "shard"), None),
        P(("mass", "shard"), None),
        P(("mass", "shard")),
    )
    return jax.shard_map(
        functools.partial(per_device, mesh.shape["mass"], mesh.shape["shard"]),
        mesh=mesh,
        in_specs=placed,
        out_specs=P(("mass", "shard"), None),
        check_vma=False,
    )
```

```python
import functools

import jax
import jax.numpy as jnp
from jax import lax
from jax.experimental import pallas as pl
from jax.experimental.pallas import tpu as pltpu
from jax.sharding import PartitionSpec as P

MESH = pl.DeviceIdType.MESH
MAX_SHIFT = 2048
TOP_K = 16
LANES = 128
PARTS = 4
F32 = jnp.float32
BF16 = jnp.bfloat16


def comparators(count):
    pairs = []
    p = 1
    while p < count:
        k = p
        while k >= 1:
            for j in range(k % p, count - k, 2 * k):
                for i in range(min(k, count - j - k)):
                    if (i + j) // (2 * p) == (i + j + k) // (2 * p):
                        pairs.append((i + j, i + j + k))
            k //= 2
        p *= 2
    return pairs


def exchange(values, pairs):
    values = list(values)
    for i, j in pairs:
        a, b = values[i], values[j]
        values[i], values[j] = jnp.maximum(a, b), jnp.minimum(a, b)
    return values


SORT = comparators(TOP_K)
BITONIC = [
    (i, i + d) for d in (8, 4, 2, 1) for i in range(TOP_K) if i & d == 0
]


def merge(first, second):
    kept = [jnp.maximum(first[i], second[TOP_K - 1 - i]) for i in range(TOP_K)]
    return exchange(kept, BITONIC)


def spectra_parts(core, queries_ref, offsets_ref, routes_ref, halves, hots, owns):
    rows, bins = queries_ref.shape
    half = bins // 2
    parts, width = halves.shape[1], halves.shape[3]
    capacity = rows // 2
    down = lax.broadcasted_iota(jnp.int32, (rows, rows), 0)
    right = lax.broadcasted_iota(jnp.int32, (rows, rows), 1)

    def as_column(row):
        spread = jnp.broadcast_to(row.astype(F32), (rows, rows))
        return jnp.sum(jnp.where(down == right, spread, 0.0), axis=1, keepdims=True).astype(
            jnp.int32
        )

    plain = queries_ref[...].astype(F32)
    margin = jnp.zeros((rows, MAX_SHIFT), F32)
    current = jnp.concatenate([margin, plain, margin], axis=1)
    start = MAX_SHIFT - as_column(offsets_ref[...])
    step = 2 * MAX_SHIFT
    current = jnp.where(
        (start & step) != 0,
        jnp.concatenate([current[:, step:], jnp.zeros((rows, step), F32)], axis=1),
        current,
    )
    step //= 2
    while step >= LANES:
        wide = bins + step
        current = jnp.where(
            (start & step) != 0, current[:, step : step + wide], current[:, :wide]
        )
        step //= 2
    wide = bins + LANES
    while step >= 1:
        moved = pltpu.roll(current, wide - step, 1)
        current = jnp.where((start & step) != 0, moved, current)
        step //= 2
    combined = plain + current[:, :bins]
    scale = lax.rsqrt(jnp.sum(combined * combined, axis=1, keepdims=True) * (1.0 / bins) + 1e-06)
    spectra = (combined * scale).astype(BF16)
    group = as_column(routes_ref[...])
    earlier = (group == routes_ref[...]) & (down > right)
    rank = jnp.sum(jnp.where(earlier, 1.0, 0.0), axis=1, keepdims=True).astype(jnp.int32)
    lane = lax.broadcasted_iota(jnp.int32, (rows, LANES), 1)
    slot = group * (2 * capacity) + core * capacity + rank
    hots[...] = jnp.where(lane == slot, 1.0, 0.0).astype(BF16)
    owns[...] = jnp.where(lane == group * capacity + rank, 1.0, 0.0)
    for side in range(2):
        for part in range(parts):
            at = side * half + part * width
            halves[side, part] = spectra[:, at : at + width]


def search_kernel(
    mass_count,
    shard_count,
    queries_ref,
    offsets_ref,
    routes_ref,
    library_ref,
    out_ref,
    plain,
    shifts,
    groups,
    halves,
    hots,
    owns,
    lib,
    held,
    held_hots,
    packed,
    slots,
    scores,
    outgoing,
    lists,
    lib_sem,
    load_sem,
    start_sem,
    hot_send,
    hot_recv,
    line_send,
    line_recv,
    layer_send,
    layer_recv,
    pair_send,
    pair_recv,
    list_send,
    list_recv,
):
    places = shard_count // 2
    parts, rows, width = halves.shape[1:]
    half = parts * width
    cap = rows // 2
    block = mass_count * rows
    total = places * block
    mass = lax.axis_index("mass")
    shard = lax.axis_index("shard")
    place = shard // 2
    core = lax.rem(shard, 2)
    sibling = (mass, shard + 1 - 2 * core)
    device_count = mass_count * shard_count
    me = mass * shard_count + shard

    loads = [
        pltpu.make_async_copy(source, target, load_sem.at[i])
        for i, (source, target) in enumerate(
            [(queries_ref, plain), (offsets_ref, shifts), (routes_ref, groups)]
        )
    ]
    for load in loads:
        load.start()
    lib_copy = pltpu.make_async_copy(library_ref, lib, lib_sem)
    barrier = pltpu.get_barrier_semaphore()

    def greet(k, carry):
        other = lax.rem(me + k, device_count)
        pl.semaphore_signal(
            barrier,
            inc=1,
            device_id=(other // shard_count, lax.rem(other, shard_count)),
            device_id_type=MESH,
        )
        return carry

    lax.fori_loop(1, device_count, greet, 0)
    for load in loads:
        load.wait()
    lib_copy.start()
    spectra_parts(core, plain, shifts, groups, halves, hots, owns)
    pl.semaphore_wait(barrier, device_count - 1)

    mine = pl.ds(pl.multiple_of(core * rows, rows), rows)
    swap = pltpu.make_async_remote_copy(
        src_ref=halves.at[1 - core],
        dst_ref=held.at[place, :, mine, :],
        send_sem=start_sem.at[0],
        recv_sem=start_sem.at[1],
        device_id=sibling,
        device_id_type=MESH,
    )
    swap.start()
    swap_hot = pltpu.make_async_remote_copy(
        src_ref=hots,
        dst_ref=held_hots.at[place, mine, :],
        send_sem=start_sem.at[3],
        recv_sem=start_sem.at[4],
        device_id=sibling,
        device_id_type=MESH,
    )
    swap_hot.start()
    keep = pltpu.make_async_copy(halves.at[core], held.at[place, :, mine, :], start_sem.at[2])
    keep.start()
    held_hots[place, mine, :] = hots[...]
    keep.wait()
    swap_hot.wait_recv()
    swap.wait_recv()

    def hot_copy(origin, way):
        return pltpu.make_async_remote_copy(
            src_ref=held_hots.at[origin],
            dst_ref=held_hots.at[origin],
            send_sem=hot_send.at[way, origin],
            recv_sem=hot_recv.at[origin],
            device_id=(mass, shard + (2 if way == 0 else -2)),
            device_id_type=MESH,
        )

    def line_copy(origin, part, way):
        return pltpu.make_async_remote_copy(
            src_ref=held.at[origin, part],
            dst_ref=held.at[origin, part],
            send_sem=line_send.at[way, origin * parts + part],
            recv_sem=line_recv.at[origin * parts + part],
            device_id=(mass, shard + (2 if way == 0 else -2)),
            device_id_type=MESH,
        )

    def layer_rows(origin, source):
        return pl.ds(pl.multiple_of(origin * block + source * rows, rows), rows)

    def layer_copy(origin, part, hop):
        target = lax.rem(mass + hop, mass_count)
        return pltpu.make_async_remote_copy(
            src_ref=packed.at[origin, part, layer_rows(0, target)],
            dst_ref=slots.at[core, part, layer_rows(origin, mass)],
            send_sem=layer_send.at[origin * parts + part, hop],
            recv_sem=layer_recv.at[origin * parts + part, hop],
            device_id=(target, shard),
            device_id_type=MESH,
        )

    def layer_arrival(origin, part, hop):
        source = lax.rem(mass + mass_count - hop, mass_count)
        return pltpu.make_async_remote_copy(
            src_ref=packed.at[origin, part, pl.ds(0, rows)],
            dst_ref=slots.at[core, part, layer_rows(origin, source)],
            send_sem=layer_send.at[origin * parts + part, hop],
            recv_sem=layer_recv.at[origin * parts + part, hop],
            device_id=(source, shard),
            device_id_type=MESH,
        )

    def pair_copy(origin, part, side):
        span = slots.at[side, part, pl.ds(pl.multiple_of(origin * block, block), block)]
        return pltpu.make_async_remote_copy(
            src_ref=span,
            dst_ref=span,
            send_sem=pair_send.at[origin * parts + part],
            recv_sem=pair_recv.at[origin * parts + part],
            device_id=sibling,
            device_id_type=MESH,
        )

    tile = min(512, width)

    def dispatch(origin, part):
        hot = held_hots[origin].astype(F32).T[:block].astype(BF16)

        def pack(j, carry):
            span = pl.ds(pl.multiple_of(j * tile, tile), tile)
            packed[origin, part, :, span] = jnp.dot(
                hot, held[origin, part, :, span], preferred_element_type=F32
            ).astype(BF16)
            return carry

        lax.fori_loop(0, width // tile, pack, 0)
        for hop in range(1, mass_count):
            layer_copy(origin, part, hop).start()
        slots[core, part, layer_rows(origin, mass), :] = packed[
            origin, part, layer_rows(0, mass), :
        ]

    def leave(part):
        for way, there in ((0, place + 1 < places), (1, place > 0)):

            @pl.when(there)
            def _():
                if part == 0:
                    hot_copy(place, way).start()
                line_copy(place, part, way).start()

    def take(origin, part, way, there):
        if part == 0:
            hot_copy(origin, way).wait_recv()
        line_copy(origin, part, way).wait_recv()

        @pl.when(there)
        def _():
            if part == 0:
                hot_copy(origin, way).start()
            line_copy(origin, part, way).start()

        dispatch(origin, part)

    def gather(part):
        if part + 2 < parts:
            leave(part + 2)
        dispatch(place, part)

        def advance(t, carry):
            below, above = place - 1 - t, place + 1 + t

            @pl.when(below >= 0)
            def _():
                take(below, part, 0, place + 1 < places)

            @pl.when(above < places)
            def _():
                take(above, part, 1, place > 0)

            return carry

        lax.fori_loop(0, places - 1, advance, 0)

    def hand_over(part):
        def one(origin):
            for hop in range(1, mass_count):
                layer_arrival(origin, part, hop).wait_recv()
            pair_copy(origin, part, core).start()

        one(place)

        def advance(t, carry):
            for origin in (place - 1 - t, place + 1 + t):

                @pl.when((origin >= 0) & (origin < places))
                def _():
                    one(origin)

            return carry

        lax.fori_loop(0, places - 1, advance, 0)

    lib_rows = lib.shape[0]
    tall, wide = min(512, lib_rows), min(256, total)

    def multiply(part):
        lax.fori_loop(
            0, places, lambda o, x: (pair_copy(o, part, 1 - core).wait_recv(), x)[1], 0
        )

        def score(k, carry):
            i, j = k // (total // wide), lax.rem(k, total // wide)
            down = pl.ds(pl.multiple_of(i * tall, tall), tall)
            across = pl.ds(pl.multiple_of(j * wide, wide), wide)
            sums = None if part == 0 else scores[down, across]
            for side in range(2):
                at = side * half + part * width
                term = lax.dot_general(
                    lib[down, at : at + width],
                    slots[side, part, across, :],
                    (((1,), (1,)), ((), ())),
                    preferred_element_type=F32,
                )
                sums = term if sums is None else sums + term
            scores[down, across] = sums
            return carry

        lax.fori_loop(0, (lib_rows // tall) * (total // wide), score, 0)

    for part in range(min(2, parts)):
        leave(part)
    for step in range(parts + 2):
        if step < parts:
            gather(step)
        if 0 <= step - 1 < parts:
            hand_over(step - 1)
        if step == 2:
            lib_copy.wait()
        if step >= 2:
            multiply(step - 2)

    sub = lax.broadcasted_iota(jnp.int32, (8, LANES), 0)

    def as_columns(values):
        upper, lower = values[0], values[8]
        for i in range(1, 8):
            upper = jnp.where(sub == i, values[i], upper)
            lower = jnp.where(sub == i, values[8 + i], lower)
        rest = jnp.zeros((LANES - TOP_K, LANES), F32)
        return jnp.concatenate([upper, lower, rest], axis=0).T

    stride = lib_rows // TOP_K

    def best(tile, carry):
        across = pl.ds(pl.multiple_of(tile * LANES, LANES), LANES)

        def more(r, kept):
            fresh = [
                scores[pl.ds(pl.multiple_of(i * stride + r * 8, 8), 8), across]
                for i in range(TOP_K)
            ]
            return tuple(merge(kept, exchange(fresh, SORT)))

        kept = tuple(jnp.full((8, LANES), -jnp.inf, F32) for _ in range(TOP_K))
        kept = lax.fori_loop(0, stride // 8, more, kept)
        for d in (4, 2, 1):
            kept = merge(kept, [pltpu.roll(x, d, 0) for x in kept])
        outgoing[across, :] = as_columns(kept)
        return carry

    lax.fori_loop(0, total // LANES, best, 0)

    def list_copy(k):
        other = lax.rem(me + k, device_count)
        to_mass, to_shard = other // shard_count, lax.rem(other, shard_count)
        at = ((to_shard // 2) * mass_count + to_mass) * 2 + lax.rem(to_shard, 2)
        return pltpu.make_async_remote_copy(
            src_ref=outgoing.at[pl.ds(pl.multiple_of(at * cap, cap), cap)],
            dst_ref=lists.at[
                pl.ds(pl.multiple_of((shard * mass_count + mass) * cap, cap), cap)
            ],
            send_sem=list_send.at[k],
            recv_sem=list_recv.at[k],
            device_id=(to_mass, to_shard),
            device_id_type=MESH,
        )

    def list_arrival(k):
        other = lax.rem(me + device_count - k, device_count)
        from_mass, from_shard = other // shard_count, lax.rem(other, shard_count)
        return pltpu.make_async_remote_copy(
            src_ref=outgoing.at[pl.ds(0, cap)],
            dst_ref=lists.at[
                pl.ds(pl.multiple_of((from_shard * mass_count + from_mass) * cap, cap), cap)
            ],
            send_sem=list_send.at[k],
            recv_sem=list_recv.at[k],
            device_id=(from_mass, from_shard),
            device_id_type=MESH,
        )

    lax.fori_loop(1, device_count, lambda k, x: (list_copy(k).start(), x)[1], 0)
    own_at = ((place * mass_count + mass) * 2 + core) * cap
    lists[pl.ds(pl.multiple_of((shard * mass_count + mass) * cap, cap), cap), :] = outgoing[
        pl.ds(pl.multiple_of(own_at, cap), cap), :
    ]
    lax.fori_loop(1, device_count, lambda k, x: (list_arrival(k).wait_recv(), x)[1], 0)

    kept = None
    for tile in range(device_count * cap // LANES):
        turned = lists[tile * LANES : (tile + 1) * LANES, :].T
        fresh = [jnp.broadcast_to(turned[i : i + 1, :], (8, LANES)) for i in range(TOP_K)]
        kept = fresh if kept is None else merge(kept, fresh)
    turn = mass_count * cap
    while turn < LANES:
        kept = merge(kept, [pltpu.roll(x, turn, 1) for x in kept])
        turn *= 2
    chosen = jnp.dot(
        owns[...],
        as_columns(kept),
        preferred_element_type=F32,
        precision=lax.Precision.HIGHEST,
    )
    out_ref[...] = chosen

    swap.wait_send()
    swap_hot.wait_send()

    def finish(origin, carry):
        for way, there in (
            (0, (place + 1 < places) & (origin <= place)),
            (1, (place > 0) & (origin >= place)),
        ):

            @pl.when(there)
            def _():
                hot_copy(origin, way).wait_send()
                for part in range(parts):
                    line_copy(origin, part, way).wait_send()

        for part in range(parts):
            for hop in range(1, mass_count):
                layer_copy(origin, part, hop).wait_send()
            pair_copy(origin, part, core).wait_send()
        return carry

    lax.fori_loop(0, places, finish, 0)
    lax.fori_loop(1, device_count, lambda k, x: (list_copy(k).wait_send(), x)[1], 0)


def per_device(mass_count, shard_count, queries, library, routes, offsets):
    rows, bins = queries.shape
    half = bins // 2
    places = shard_count // 2
    cap = rows // 2
    block = mass_count * rows
    total = places * block
    device_count = mass_count * shard_count
    width = half // PARTS
    anywhere = pl.BlockSpec(memory_space=pl.ANY)
    dma = pltpu.SemaphoreType.DMA
    best = pl.pallas_call(
        functools.partial(search_kernel, mass_count, shard_count),
        out_shape=jax.ShapeDtypeStruct((rows, LANES), F32),
        in_specs=[anywhere] * 4,
        out_specs=pl.BlockSpec(memory_space=pltpu.VMEM),
        scratch_shapes=[
            pltpu.VMEM((rows, bins), BF16),
            pltpu.VMEM((1, rows), jnp.int32),
            pltpu.VMEM((1, rows), jnp.int32),
            pltpu.VMEM((2, PARTS, rows, width), BF16),
            pltpu.VMEM((rows, LANES), BF16),
            pltpu.VMEM((rows, LANES), F32),
            pltpu.VMEM(library.shape, BF16),
            pltpu.VMEM((places, PARTS, 2 * rows, width), BF16),
            pltpu.VMEM((places, 2 * rows, LANES), BF16),
            pltpu.VMEM((places, PARTS, block, width), BF16),
            pltpu.VMEM((2, PARTS, total, width), BF16),
            pltpu.VMEM((library.shape[0], total), F32),
            pltpu.VMEM((total, LANES), F32),
            pltpu.VMEM((device_count * cap, LANES), F32),
            dma,
            dma((3,)),
            dma((5,)),
            dma((2, places)),
            dma((places,)),
            dma((2, places * PARTS)),
            dma((places * PARTS,)),
            dma((places * PARTS, mass_count)),
            dma((places * PARTS, mass_count)),
            dma((places * PARTS,)),
            dma((places * PARTS,)),
            dma((device_count,)),
            dma((device_count,)),
        ],
        compiler_params=pltpu.CompilerParams(
            collective_id=0, has_side_effects=True, vmem_limit_bytes=56 * 2**20
        ),
    )(queries, offsets.reshape(1, rows), routes.reshape(1, rows), library)
    return best[:, :TOP_K]


def solution(mesh):
    placed = (
        P(("mass", "shard"), None),
        P(("mass", "shard"), None),
        P(("mass", "shard"), None),
        P(("mass", "shard")),
    )
    return jax.shard_map(
        functools.partial(per_device, mesh.shape["mass"], mesh.shape["shard"]),
        mesh=mesh,
        in_specs=placed,
        out_specs=P(("mass", "shard"), None),
        check_vma=False,
    )
```

```python
import functools

import jax
import jax.numpy as jnp
from jax import lax
from jax.experimental import pallas as pl
from jax.experimental.pallas import tpu as pltpu
from jax.sharding import PartitionSpec as P

MESH = pl.DeviceIdType.MESH
MAX_SHIFT = 2048
TOP_K = 16
LANES = 128
PARTS = 4
F32 = jnp.float32
BF16 = jnp.bfloat16


def comparators(count):
    pairs = []
    p = 1
    while p < count:
        k = p
        while k >= 1:
            for j in range(k % p, count - k, 2 * k):
                for i in range(min(k, count - j - k)):
                    if (i + j) // (2 * p) == (i + j + k) // (2 * p):
                        pairs.append((i + j, i + j + k))
            k //= 2
        p *= 2
    return pairs


def exchange(values, pairs):
    values = list(values)
    for i, j in pairs:
        a, b = values[i], values[j]
        values[i], values[j] = jnp.maximum(a, b), jnp.minimum(a, b)
    return values


SORT = comparators(TOP_K)
BITONIC = [
    (i, i + d) for d in (8, 4, 2, 1) for i in range(TOP_K) if i & d == 0
]


def merge(first, second):
    kept = [jnp.maximum(first[i], second[TOP_K - 1 - i]) for i in range(TOP_K)]
    return exchange(kept, BITONIC)


def spectra_parts(core, queries_ref, offsets_ref, routes_ref, halves, hots, owns):
    rows, bins = queries_ref.shape
    half = bins // 2
    parts, width = halves.shape[1], halves.shape[3]
    capacity = rows // 2
    down = lax.broadcasted_iota(jnp.int32, (rows, rows), 0)
    right = lax.broadcasted_iota(jnp.int32, (rows, rows), 1)

    def as_column(row):
        spread = jnp.broadcast_to(row.astype(F32), (rows, rows))
        return jnp.sum(jnp.where(down == right, spread, 0.0), axis=1, keepdims=True).astype(
            jnp.int32
        )

    plain = queries_ref[...].astype(F32)
    margin = jnp.zeros((rows, MAX_SHIFT), F32)
    current = jnp.concatenate([margin, plain, margin], axis=1)
    start = MAX_SHIFT - as_column(offsets_ref[...])
    step = 2 * MAX_SHIFT
    current = jnp.where(
        (start & step) != 0,
        jnp.concatenate([current[:, step:], jnp.zeros((rows, step), F32)], axis=1),
        current,
    )
    step //= 2
    while step >= LANES:
        wide = bins + step
        current = jnp.where(
            (start & step) != 0, current[:, step : step + wide], current[:, :wide]
        )
        step //= 2
    wide = bins + LANES
    while step >= 1:
        moved = pltpu.roll(current, wide - step, 1)
        current = jnp.where((start & step) != 0, moved, current)
        step //= 2
    combined = plain + current[:, :bins]
    scale = lax.rsqrt(jnp.sum(combined * combined, axis=1, keepdims=True) * (1.0 / bins) + 1e-06)
    spectra = (combined * scale).astype(BF16)
    group = as_column(routes_ref[...])
    earlier = (group == routes_ref[...]) & (down > right)
    rank = jnp.sum(jnp.where(earlier, 1.0, 0.0), axis=1, keepdims=True).astype(jnp.int32)
    lane = lax.broadcasted_iota(jnp.int32, (rows, LANES), 1)
    slot = group * (2 * capacity) + core * capacity + rank
    hots[...] = jnp.where(lane == slot, 1.0, 0.0).astype(BF16)
    owns[...] = jnp.where(lane == group * capacity + rank, 1.0, 0.0)
    for side in range(2):
        for part in range(parts):
            at = side * half + part * width
            halves[side, part] = spectra[:, at : at + width]


def search_kernel(
    mass_count,
    shard_count,
    queries_ref,
    offsets_ref,
    routes_ref,
    library_ref,
    out_ref,
    plain,
    shifts,
    groups,
    halves,
    hots,
    owns,
    lib,
    held,
    held_hots,
    packed,
    slots,
    scores,
    outgoing,
    lists,
    merged,
    homes,
    lib_sem,
    load_sem,
    start_sem,
    hot_send,
    hot_recv,
    line_send,
    line_recv,
    layer_send,
    layer_recv,
    pair_send,
    pair_recv,
    list_send,
    list_recv,
    home_send,
    home_recv,
):
    places = shard_count // 2
    parts, rows, width = halves.shape[1:]
    half = parts * width
    cap = rows // 2
    block = mass_count * rows
    total = places * block
    mass = lax.axis_index("mass")
    shard = lax.axis_index("shard")
    place = shard // 2
    core = lax.rem(shard, 2)
    sibling = (mass, shard + 1 - 2 * core)

    loads = [
        pltpu.make_async_copy(source, target, load_sem.at[i])
        for i, (source, target) in enumerate(
            [(queries_ref, plain), (offsets_ref, shifts), (routes_ref, groups)]
        )
    ]
    for load in loads:
        load.start()
    lib_copy = pltpu.make_async_copy(library_ref, lib, lib_sem)
    barrier = pltpu.get_barrier_semaphore()

    def greet(device):
        pl.semaphore_signal(barrier, inc=1, device_id=device, device_id_type=MESH)

    def mass_peer(k):
        return (lax.rem(mass + k, mass_count), shard)

    def shard_peer(k):
        return (mass, lax.rem(shard + k, shard_count))

    for k in range(1, mass_count):
        greet(mass_peer(k))
    for k in range(1, shard_count):
        greet(shard_peer(k))
    for load in loads:
        load.wait()
    lib_copy.start()
    spectra_parts(core, plain, shifts, groups, halves, hots, owns)
    pl.semaphore_wait(barrier, mass_count + shard_count - 2)

    mine = pl.ds(pl.multiple_of(core * rows, rows), rows)
    swap = pltpu.make_async_remote_copy(
        src_ref=halves.at[1 - core],
        dst_ref=held.at[place, :, mine, :],
        send_sem=start_sem.at[0],
        recv_sem=start_sem.at[1],
        device_id=sibling,
        device_id_type=MESH,
    )
    swap.start()
    swap_hot = pltpu.make_async_remote_copy(
        src_ref=hots,
        dst_ref=held_hots.at[place, mine, :],
        send_sem=start_sem.at[3],
        recv_sem=start_sem.at[4],
        device_id=sibling,
        device_id_type=MESH,
    )
    swap_hot.start()
    keep = pltpu.make_async_copy(halves.at[core], held.at[place, :, mine, :], start_sem.at[2])
    keep.start()
    held_hots[place, mine, :] = hots[...]
    keep.wait()
    swap_hot.wait_recv()
    swap.wait_recv()

    def hot_copy(origin, way):
        return pltpu.make_async_remote_copy(
            src_ref=held_hots.at[origin],
            dst_ref=held_hots.at[origin],
            send_sem=hot_send.at[way, origin],
            recv_sem=hot_recv.at[origin],
            device_id=(mass, shard + (2 if way == 0 else -2)),
            device_id_type=MESH,
        )

    def line_copy(origin, part, way):
        return pltpu.make_async_remote_copy(
            src_ref=held.at[origin, part],
            dst_ref=held.at[origin, part],
            send_sem=line_send.at[way, origin * parts + part],
            recv_sem=line_recv.at[origin * parts + part],
            device_id=(mass, shard + (2 if way == 0 else -2)),
            device_id_type=MESH,
        )

    def layer_rows(origin, source):
        return pl.ds(pl.multiple_of(origin * block + source * rows, rows), rows)

    def layer_copy(origin, part, hop):
        target = lax.rem(mass + hop, mass_count)
        return pltpu.make_async_remote_copy(
            src_ref=packed.at[origin, part, layer_rows(0, target)],
            dst_ref=slots.at[core, part, layer_rows(origin, mass)],
            send_sem=layer_send.at[origin * parts + part, hop],
            recv_sem=layer_recv.at[origin * parts + part, hop],
            device_id=(target, shard),
            device_id_type=MESH,
        )

    def layer_arrival(origin, part, hop):
        source = lax.rem(mass + mass_count - hop, mass_count)
        return pltpu.make_async_remote_copy(
            src_ref=packed.at[origin, part, pl.ds(0, rows)],
            dst_ref=slots.at[core, part, layer_rows(origin, source)],
            send_sem=layer_send.at[origin * parts + part, hop],
            recv_sem=layer_recv.at[origin * parts + part, hop],
            device_id=(source, shard),
            device_id_type=MESH,
        )

    def pair_copy(origin, part, side):
        span = slots.at[side, part, pl.ds(pl.multiple_of(origin * block, block), block)]
        return pltpu.make_async_remote_copy(
            src_ref=span,
            dst_ref=span,
            send_sem=pair_send.at[origin * parts + part],
            recv_sem=pair_recv.at[origin * parts + part],
            device_id=sibling,
            device_id_type=MESH,
        )

    tile = min(512, width)

    def dispatch(origin, part):
        hot = held_hots[origin].astype(F32).T[:block].astype(BF16)

        def pack(j, carry):
            span = pl.ds(pl.multiple_of(j * tile, tile), tile)
            packed[origin, part, :, span] = jnp.dot(
                hot, held[origin, part, :, span], preferred_element_type=F32
            ).astype(BF16)
            return carry

        lax.fori_loop(0, width // tile, pack, 0)
        for hop in range(1, mass_count):
            layer_copy(origin, part, hop).start()
        slots[core, part, layer_rows(origin, mass), :] = packed[
            origin, part, layer_rows(0, mass), :
        ]

    def leave(part):
        for way, there in ((0, place + 1 < places), (1, place > 0)):

            @pl.when(there)
            def _():
                if part == 0:
                    hot_copy(place, way).start()
                line_copy(place, part, way).start()

    def take(origin, part, way, there):
        if part == 0:
            hot_copy(origin, way).wait_recv()
        line_copy(origin, part, way).wait_recv()

        @pl.when(there)
        def _():
            if part == 0:
                hot_copy(origin, way).start()
            line_copy(origin, part, way).start()

        dispatch(origin, part)

    def hop(part, t):
        below, above = place - 1 - t, place + 1 + t

        @pl.when(below >= 0)
        def _():
            take(below, part, 0, place + 1 < places)

        @pl.when(above < places)
        def _():
            take(above, part, 1, place > 0)

    def hand_over(part):
        def one(origin):
            for hop in range(1, mass_count):
                layer_arrival(origin, part, hop).wait_recv()
            pair_copy(origin, part, core).start()

        one(place)

        def advance(t, carry):
            for origin in (place - 1 - t, place + 1 + t):

                @pl.when((origin >= 0) & (origin < places))
                def _():
                    one(origin)

            return carry

        lax.fori_loop(0, places - 1, advance, 0)

    lib_rows = lib.shape[0]
    tall, wide = min(512, lib_rows), min(256, total)

    def multiply(part):
        lax.fori_loop(
            0, places, lambda o, x: (pair_copy(o, part, 1 - core).wait_recv(), x)[1], 0
        )

        def score(k, carry):
            i, j = k // (total // wide), lax.rem(k, total // wide)
            down = pl.ds(pl.multiple_of(i * tall, tall), tall)
            across = pl.ds(pl.multiple_of(j * wide, wide), wide)
            sums = None if part == 0 else scores[down, across]
            for side in range(2):
                at = side * half + part * width
                term = lax.dot_general(
                    lib[down, at : at + width],
                    slots[side, part, across, :],
                    (((1,), (1,)), ((), ())),
                    preferred_element_type=F32,
                )
                sums = term if sums is None else sums + term
            scores[down, across] = sums
            return carry

        lax.fori_loop(0, (lib_rows // tall) * (total // wide), score, 0)

    for part in range(min(2, parts)):
        leave(part)

    def fill(step, carry):
        for part in range(2, parts):

            @pl.when(step == part - 2)
            def _():
                leave(part)

        for part in range(parts):

            @pl.when((step > part) & (step - part < places))
            def _():
                hop(part, step - 1 - part)

            @pl.when(step == part)
            def _():
                dispatch(place, part)

        return carry

    steady = max(places, parts)
    lax.fori_loop(0, steady, fill, 0)
    for step in range(steady, steady + parts + 1):
        for part in range(parts):
            if 0 <= step - 1 - part < places - 1:
                hop(part, step - 1 - part)
        if step - steady < parts:
            hand_over(step - steady)
        if step == steady + 1:
            lib_copy.wait()
        if step > steady:
            multiply(step - steady - 1)

    sub = lax.broadcasted_iota(jnp.int32, (8, LANES), 0)

    def as_columns(values):
        upper, lower = values[0], values[8]
        for i in range(1, 8):
            upper = jnp.where(sub == i, values[i], upper)
            lower = jnp.where(sub == i, values[8 + i], lower)
        rest = jnp.zeros((LANES - TOP_K, LANES), F32)
        return jnp.concatenate([upper, lower, rest], axis=0).T

    stride = lib_rows // TOP_K

    def best(tile, carry):
        across = pl.ds(pl.multiple_of(tile * LANES, LANES), LANES)

        def more(r, kept):
            fresh = [
                scores[pl.ds(pl.multiple_of(i * stride + r * 8, 8), 8), across]
                for i in range(TOP_K)
            ]
            return tuple(merge(kept, exchange(fresh, SORT)))

        kept = tuple(jnp.full((8, LANES), -jnp.inf, F32) for _ in range(TOP_K))
        kept = lax.fori_loop(0, stride // 8, more, kept)
        for d in (4, 2, 1):
            kept = merge(kept, [pltpu.roll(x, d, 0) for x in kept])
        columns = as_columns(kept)
        for i in range(LANES // block):
            for m in range(mass_count):
                for c in range(2):
                    at = i * block + m * rows + c * cap
                    outgoing[tile * (LANES // block) + i, c, m * cap : (m + 1) * cap, :] = columns[
                        at : at + cap
                    ]
        return carry

    lax.fori_loop(0, total // LANES, best, 0)

    list_rows = mass_count * cap

    def list_copy(k):
        target = shard_peer(k)
        return pltpu.make_async_remote_copy(
            src_ref=outgoing.at[target[1] // 2, lax.rem(target[1], 2)],
            dst_ref=lists.at[pl.ds(pl.multiple_of(shard * list_rows, list_rows), list_rows)],
            send_sem=list_send.at[k],
            recv_sem=list_recv.at[k],
            device_id=target,
            device_id_type=MESH,
        )

    def list_arrival(k):
        source = shard_peer(shard_count - k)
        return pltpu.make_async_remote_copy(
            src_ref=outgoing.at[0, 0],
            dst_ref=lists.at[pl.ds(pl.multiple_of(source[1] * list_rows, list_rows), list_rows)],
            send_sem=list_send.at[k],
            recv_sem=list_recv.at[k],
            device_id=source,
            device_id_type=MESH,
        )

    for k in range(1, shard_count):
        list_copy(k).start()
    lists[pl.ds(pl.multiple_of(shard * list_rows, list_rows), list_rows), :] = outgoing[
        place, core
    ]
    for k in range(1, shard_count):
        list_arrival(k).wait_recv()

    kept = None
    for tile in range(shard_count * list_rows // LANES):
        turned = lists[tile * LANES : (tile + 1) * LANES, :].T
        fresh = [jnp.broadcast_to(turned[i : i + 1, :], (8, LANES)) for i in range(TOP_K)]
        kept = fresh if kept is None else merge(kept, fresh)
    turn = list_rows
    while turn < LANES:
        kept = merge(kept, [pltpu.roll(x, turn, 1) for x in kept])
        turn *= 2
    merged[...] = as_columns(kept)[:list_rows]

    def group_rows(m):
        return pl.ds(pl.multiple_of(m * cap, cap), cap)

    def home_copy(k):
        target = mass_peer(k)
        return pltpu.make_async_remote_copy(
            src_ref=merged.at[group_rows(target[0])],
            dst_ref=homes.at[group_rows(mass)],
            send_sem=home_send.at[k],
            recv_sem=home_recv.at[k],
            device_id=target,
            device_id_type=MESH,
        )

    def home_arrival(k):
        source = mass_peer(mass_count - k)
        return pltpu.make_async_remote_copy(
            src_ref=merged.at[pl.ds(0, cap)],
            dst_ref=homes.at[group_rows(source[0])],
            send_sem=home_send.at[k],
            recv_sem=home_recv.at[k],
            device_id=source,
            device_id_type=MESH,
        )

    for k in range(1, mass_count):
        home_copy(k).start()
    homes[group_rows(mass), :] = merged[group_rows(mass), :]
    for k in range(1, mass_count):
        home_arrival(k).wait_recv()
    chosen = jnp.dot(
        owns[:, :list_rows],
        homes[...],
        preferred_element_type=F32,
        precision=lax.Precision.HIGHEST,
    )
    out_ref[...] = chosen

    swap.wait_send()
    swap_hot.wait_send()

    def finish(origin, carry):
        for way, there in (
            (0, (place + 1 < places) & (origin <= place)),
            (1, (place > 0) & (origin >= place)),
        ):

            @pl.when(there)
            def _():
                hot_copy(origin, way).wait_send()
                for part in range(parts):
                    line_copy(origin, part, way).wait_send()

        for part in range(parts):
            for hop in range(1, mass_count):
                layer_copy(origin, part, hop).wait_send()
            pair_copy(origin, part, core).wait_send()
        return carry

    lax.fori_loop(0, places, finish, 0)
    for k in range(1, shard_count):
        list_copy(k).wait_send()
    for k in range(1, mass_count):
        home_copy(k).wait_send()


def per_device(mass_count, shard_count, queries, library, routes, offsets):
    rows, bins = queries.shape
    half = bins // 2
    places = shard_count // 2
    cap = rows // 2
    block = mass_count * rows
    total = places * block
    width = half // PARTS
    anywhere = pl.BlockSpec(memory_space=pl.ANY)
    dma = pltpu.SemaphoreType.DMA
    best = pl.pallas_call(
        functools.partial(search_kernel, mass_count, shard_count),
        out_shape=jax.ShapeDtypeStruct((rows, LANES), F32),
        in_specs=[anywhere] * 4,
        out_specs=pl.BlockSpec(memory_space=pltpu.VMEM),
        scratch_shapes=[
            pltpu.VMEM((rows, bins), BF16),
            pltpu.VMEM((1, rows), jnp.int32),
            pltpu.VMEM((1, rows), jnp.int32),
            pltpu.VMEM((2, PARTS, rows, width), BF16),
            pltpu.VMEM((rows, LANES), BF16),
            pltpu.VMEM((rows, LANES), F32),
            pltpu.VMEM(library.shape, BF16),
            pltpu.VMEM((places, PARTS, 2 * rows, width), BF16),
            pltpu.VMEM((places, 2 * rows, LANES), BF16),
            pltpu.VMEM((places, PARTS, block, width), BF16),
            pltpu.VMEM((2, PARTS, total, width), BF16),
            pltpu.VMEM((library.shape[0], total), F32),
            pltpu.VMEM((places, 2, mass_count * cap, LANES), F32),
            pltpu.VMEM((shard_count * mass_count * cap, LANES), F32),
            pltpu.VMEM((mass_count * cap, LANES), F32),
            pltpu.VMEM((mass_count * cap, LANES), F32),
            dma,
            dma((3,)),
            dma((5,)),
            dma((2, places)),
            dma((places,)),
            dma((2, places * PARTS)),
            dma((places * PARTS,)),
            dma((places * PARTS, mass_count)),
            dma((places * PARTS, mass_count)),
            dma((places * PARTS,)),
            dma((places * PARTS,)),
            dma((shard_count,)),
            dma((shard_count,)),
            dma((mass_count,)),
            dma((mass_count,)),
        ],
        compiler_params=pltpu.CompilerParams(
            collective_id=0, has_side_effects=True, vmem_limit_bytes=56 * 2**20
        ),
    )(queries, offsets.reshape(1, rows), routes.reshape(1, rows), library)
    return best[:, :TOP_K]


def solution(mesh):
    placed = (
        P(("mass", "shard"), None),
        P(("mass", "shard"), None),
        P(("mass", "shard"), None),
        P(("mass", "shard")),
    )
    return jax.shard_map(
        functools.partial(per_device, mesh.shape["mass"], mesh.shape["shard"]),
        mesh=mesh,
        in_specs=placed,
        out_specs=P(("mass", "shard"), None),
        check_vma=False,
    )
```

```python
import functools

import jax
import jax.numpy as jnp
from jax import lax
from jax.experimental import pallas as pl
from jax.experimental.pallas import tpu as pltpu
from jax.sharding import PartitionSpec as P

MESH = pl.DeviceIdType.MESH
MAX_SHIFT = 2048
TOP_K = 16
LANES = 128
PARTS = 4
F32 = jnp.float32
BF16 = jnp.bfloat16


def comparators(count):
    pairs = []
    p = 1
    while p < count:
        k = p
        while k >= 1:
            for j in range(k % p, count - k, 2 * k):
                for i in range(min(k, count - j - k)):
                    if (i + j) // (2 * p) == (i + j + k) // (2 * p):
                        pairs.append((i + j, i + j + k))
            k //= 2
        p *= 2
    return pairs


def exchange(values, pairs):
    values = list(values)
    for i, j in pairs:
        a, b = values[i], values[j]
        values[i], values[j] = jnp.maximum(a, b), jnp.minimum(a, b)
    return values


SORT = comparators(TOP_K)
BITONIC = [
    (i, i + d) for d in (8, 4, 2, 1) for i in range(TOP_K) if i & d == 0
]


def merge(first, second):
    kept = [jnp.maximum(first[i], second[TOP_K - 1 - i]) for i in range(TOP_K)]
    return exchange(kept, BITONIC)


def spectra_parts(core, queries_ref, offsets_ref, routes_ref, halves, hots, owns):
    rows, bins = queries_ref.shape
    half = bins // 2
    parts, width = halves.shape[1], halves.shape[3]
    capacity = rows // 2
    down = lax.broadcasted_iota(jnp.int32, (rows, rows), 0)
    right = lax.broadcasted_iota(jnp.int32, (rows, rows), 1)

    def as_column(row):
        spread = jnp.broadcast_to(row.astype(F32), (rows, rows))
        return jnp.sum(jnp.where(down == right, spread, 0.0), axis=1, keepdims=True).astype(
            jnp.int32
        )

    plain = queries_ref[...].astype(F32)
    margin = jnp.zeros((rows, MAX_SHIFT), F32)
    current = jnp.concatenate([margin, plain, margin], axis=1)
    start = MAX_SHIFT - as_column(offsets_ref[...])
    step = 2 * MAX_SHIFT
    current = jnp.where(
        (start & step) != 0,
        jnp.concatenate([current[:, step:], jnp.zeros((rows, step), F32)], axis=1),
        current,
    )
    step //= 2
    while step >= LANES:
        wide = bins + step
        current = jnp.where(
            (start & step) != 0, current[:, step : step + wide], current[:, :wide]
        )
        step //= 2
    wide = bins + LANES
    while step >= 1:
        moved = pltpu.roll(current, wide - step, 1)
        current = jnp.where((start & step) != 0, moved, current)
        step //= 2
    combined = plain + current[:, :bins]
    scale = lax.rsqrt(jnp.sum(combined * combined, axis=1, keepdims=True) * (1.0 / bins) + 1e-06)
    spectra = (combined * scale).astype(BF16)
    group = as_column(routes_ref[...])
    earlier = (group == routes_ref[...]) & (down > right)
    rank = jnp.sum(jnp.where(earlier, 1.0, 0.0), axis=1, keepdims=True).astype(jnp.int32)
    lane = lax.broadcasted_iota(jnp.int32, (rows, LANES), 1)
    slot = group * (2 * capacity) + core * capacity + rank
    hots[...] = jnp.where(lane == slot, 1.0, 0.0).astype(BF16)
    owns[...] = jnp.where(lane == group * capacity + rank, 1.0, 0.0)
    for side in range(2):
        for part in range(parts):
            at = side * half + part * width
            halves[side, part] = spectra[:, at : at + width]


def search_kernel(
    mass_count,
    shard_count,
    queries_ref,
    offsets_ref,
    routes_ref,
    library_ref,
    out_ref,
    plain,
    shifts,
    groups,
    halves,
    hots,
    owns,
    lib,
    held,
    held_hots,
    packed,
    slots,
    scores,
    outgoing,
    lists,
    merged,
    homes,
    lib_sem,
    load_sem,
    start_sem,
    hot_send,
    hot_recv,
    line_send,
    line_recv,
    layer_send,
    layer_recv,
    pair_send,
    pair_recv,
    list_send,
    list_recv,
    home_send,
    home_recv,
):
    places = shard_count // 2
    parts, rows, width = halves.shape[1:]
    half = parts * width
    cap = rows // 2
    block = mass_count * rows
    total = places * block
    mass = lax.axis_index("mass")
    shard = lax.axis_index("shard")
    place = shard // 2
    core = lax.rem(shard, 2)
    sibling = (mass, shard + 1 - 2 * core)

    loads = [
        pltpu.make_async_copy(source, target, load_sem.at[i])
        for i, (source, target) in enumerate(
            [(queries_ref, plain), (offsets_ref, shifts), (routes_ref, groups)]
        )
    ]
    for load in loads:
        load.start()
    lib_copy = pltpu.make_async_copy(library_ref, lib, lib_sem)
    barrier = pltpu.get_barrier_semaphore()

    def greet(device):
        pl.semaphore_signal(barrier, inc=1, device_id=device, device_id_type=MESH)

    def mass_peer(k):
        return (lax.rem(mass + k, mass_count), shard)

    def shard_peer(k):
        return (mass, lax.rem(shard + k, shard_count))

    for k in range(1, mass_count):
        greet(mass_peer(k))
    for k in range(1, shard_count):
        greet(shard_peer(k))
    for load in loads:
        load.wait()
    lib_copy.start()
    spectra_parts(core, plain, shifts, groups, halves, hots, owns)
    pl.semaphore_wait(barrier, mass_count + shard_count - 2)

    mine = pl.ds(pl.multiple_of(core * rows, rows), rows)
    swap = pltpu.make_async_remote_copy(
        src_ref=halves.at[1 - core],
        dst_ref=held.at[place, :, mine, :],
        send_sem=start_sem.at[0],
        recv_sem=start_sem.at[1],
        device_id=sibling,
        device_id_type=MESH,
    )
    swap.start()
    swap_hot = pltpu.make_async_remote_copy(
        src_ref=hots,
        dst_ref=held_hots.at[place, mine, :],
        send_sem=start_sem.at[3],
        recv_sem=start_sem.at[4],
        device_id=sibling,
        device_id_type=MESH,
    )
    swap_hot.start()
    keep = pltpu.make_async_copy(halves.at[core], held.at[place, :, mine, :], start_sem.at[2])
    keep.start()
    held_hots[place, mine, :] = hots[...]
    keep.wait()
    swap_hot.wait_recv()
    swap.wait_recv()

    def hot_copy(origin, way):
        return pltpu.make_async_remote_copy(
            src_ref=held_hots.at[origin],
            dst_ref=held_hots.at[origin],
            send_sem=hot_send.at[way, origin],
            recv_sem=hot_recv.at[origin],
            device_id=(mass, shard + (2 if way == 0 else -2)),
            device_id_type=MESH,
        )

    def line_copy(origin, part, way):
        return pltpu.make_async_remote_copy(
            src_ref=held.at[origin, part],
            dst_ref=held.at[origin, part],
            send_sem=line_send.at[way, origin * parts + part],
            recv_sem=line_recv.at[origin * parts + part],
            device_id=(mass, shard + (2 if way == 0 else -2)),
            device_id_type=MESH,
        )

    def layer_rows(origin, source):
        return pl.ds(pl.multiple_of(origin * block + source * rows, rows), rows)

    def layer_copy(origin, part, hop):
        target = lax.rem(mass + hop, mass_count)
        return pltpu.make_async_remote_copy(
            src_ref=packed.at[origin, part, layer_rows(0, target)],
            dst_ref=slots.at[core, part, layer_rows(origin, mass)],
            send_sem=layer_send.at[origin * parts + part, hop],
            recv_sem=layer_recv.at[origin * parts + part, hop],
            device_id=(target, shard),
            device_id_type=MESH,
        )

    def layer_arrival(origin, part, hop):
        source = lax.rem(mass + mass_count - hop, mass_count)
        return pltpu.make_async_remote_copy(
            src_ref=packed.at[origin, part, pl.ds(0, rows)],
            dst_ref=slots.at[core, part, layer_rows(origin, source)],
            send_sem=layer_send.at[origin * parts + part, hop],
            recv_sem=layer_recv.at[origin * parts + part, hop],
            device_id=(source, shard),
            device_id_type=MESH,
        )

    def pair_copy(origin, part, side):
        span = slots.at[side, part, pl.ds(pl.multiple_of(origin * block, block), block)]
        return pltpu.make_async_remote_copy(
            src_ref=span,
            dst_ref=span,
            send_sem=pair_send.at[origin * parts + part],
            recv_sem=pair_recv.at[origin * parts + part],
            device_id=sibling,
            device_id_type=MESH,
        )

    tile = min(512, width)

    def dispatch(origin, part):
        hot = held_hots[origin].astype(F32).T[:block].astype(BF16)

        def pack(j, carry):
            span = pl.ds(pl.multiple_of(j * tile, tile), tile)
            packed[origin, part, :, span] = jnp.dot(
                hot, held[origin, part, :, span], preferred_element_type=F32
            ).astype(BF16)
            return carry

        lax.fori_loop(0, width // tile, pack, 0)
        for hop in range(1, mass_count):
            layer_copy(origin, part, hop).start()
        slots[core, part, layer_rows(origin, mass), :] = packed[
            origin, part, layer_rows(0, mass), :
        ]

    def leave(part):
        for way, there in ((0, place + 1 < places), (1, place > 0)):

            @pl.when(there)
            def _():
                if part == 0:
                    hot_copy(place, way).start()
                line_copy(place, part, way).start()

    def take(origin, part, way, there):
        if part == 0:
            hot_copy(origin, way).wait_recv()
        line_copy(origin, part, way).wait_recv()

        @pl.when(there)
        def _():
            if part == 0:
                hot_copy(origin, way).start()
            line_copy(origin, part, way).start()

        dispatch(origin, part)

    def hop(part, t):
        below, above = place - 1 - t, place + 1 + t

        @pl.when(below >= 0)
        def _():
            take(below, part, 0, place + 1 < places)

        @pl.when(above < places)
        def _():
            take(above, part, 1, place > 0)

    def slots_copy(origin, part, way):
        span = slots.at[core, part, pl.ds(pl.multiple_of(origin * block, block), block)]
        return pltpu.make_async_remote_copy(
            src_ref=span,
            dst_ref=span,
            send_sem=line_send.at[way, origin * parts + part],
            recv_sem=line_recv.at[origin * parts + part],
            device_id=(mass, shard + (2 if way == 0 else -2)),
            device_id_type=MESH,
        )

    def leave_slots(part):
        for hop in range(1, mass_count):
            layer_arrival(place, part, hop).wait_recv()
        for way, there in ((0, place + 1 < places), (1, place > 0)):

            @pl.when(there)
            def _():
                slots_copy(place, part, way).start()

        pair_copy(place, part, core).start()

    def take_slots(origin, part, way, there):
        slots_copy(origin, part, way).wait_recv()

        @pl.when(there)
        def _():
            slots_copy(origin, part, way).start()

        pair_copy(origin, part, core).start()

    def hop_slots(part, t):
        below, above = place - 1 - t, place + 1 + t

        @pl.when(below >= 0)
        def _():
            take_slots(below, part, 0, place + 1 < places)

        @pl.when(above < places)
        def _():
            take_slots(above, part, 1, place > 0)

    def hand_over(part):
        def one(origin):
            for hop in range(1, mass_count):
                layer_arrival(origin, part, hop).wait_recv()
            pair_copy(origin, part, core).start()

        one(place)

        def advance(t, carry):
            for origin in (place - 1 - t, place + 1 + t):

                @pl.when((origin >= 0) & (origin < places))
                def _():
                    one(origin)

            return carry

        lax.fori_loop(0, places - 1, advance, 0)

    lib_rows = lib.shape[0]
    tall, wide = min(512, lib_rows), min(256, total)

    def multiply(part):
        lax.fori_loop(
            0, places, lambda o, x: (pair_copy(o, part, 1 - core).wait_recv(), x)[1], 0
        )

        def score(k, carry):
            i, j = k // (total // wide), lax.rem(k, total // wide)
            down = pl.ds(pl.multiple_of(i * tall, tall), tall)
            across = pl.ds(pl.multiple_of(j * wide, wide), wide)
            sums = None if part == 0 else scores[down, across]
            for side in range(2):
                at = side * half + part * width
                term = lax.dot_general(
                    lib[down, at : at + width],
                    slots[side, part, across, :],
                    (((1,), (1,)), ((), ())),
                    preferred_element_type=F32,
                )
                sums = term if sums is None else sums + term
            scores[down, across] = sums
            return carry

        lax.fori_loop(0, (lib_rows // tall) * (total // wide), score, 0)

    for part in range(2):
        leave(part)

    turned = parts - 1
    dispatch(place, turned)

    def fill(step, carry):
        for part in range(2, turned):

            @pl.when(step == part - 2)
            def _():
                leave(part)

        for part in range(turned):

            @pl.when((step > part) & (step - part < places))
            def _():
                hop(part, step - 1 - part)

            @pl.when(step == part)
            def _():
                dispatch(place, part)

        @pl.when(step == 1)
        def _():
            leave_slots(turned)

        @pl.when((step > 1) & (step - 2 < places - 1))
        def _():
            hop_slots(turned, step - 2)

        return carry

    steady = max(places, parts)
    lax.fori_loop(0, steady, fill, 0)
    for step in range(steady, steady + turned + 1):
        for part in range(turned):
            if 0 <= step - 1 - part < places - 1:
                hop(part, step - 1 - part)
        if step - 2 < places - 1:
            hop_slots(turned, step - 2)
        if step - steady < turned:
            hand_over(step - steady)
        if step == steady + 1:
            lib_copy.wait()
        if step == steady + turned:
            multiply(turned)
        if step > steady:
            multiply(step - steady - 1)

    sub = lax.broadcasted_iota(jnp.int32, (8, LANES), 0)

    def as_columns(values):
        upper, lower = values[0], values[8]
        for i in range(1, 8):
            upper = jnp.where(sub == i, values[i], upper)
            lower = jnp.where(sub == i, values[8 + i], lower)
        rest = jnp.zeros((LANES - TOP_K, LANES), F32)
        return jnp.concatenate([upper, lower, rest], axis=0).T

    stride = lib_rows // TOP_K

    def best(tile, carry):
        across = pl.ds(pl.multiple_of(tile * LANES, LANES), LANES)

        def more(r, kept):
            fresh = [
                scores[pl.ds(pl.multiple_of(i * stride + r * 8, 8), 8), across]
                for i in range(TOP_K)
            ]
            return tuple(merge(kept, exchange(fresh, SORT)))

        kept = tuple(jnp.full((8, LANES), -jnp.inf, F32) for _ in range(TOP_K))
        kept = lax.fori_loop(0, stride // 8, more, kept)
        for d in (4, 2, 1):
            kept = merge(kept, [pltpu.roll(x, d, 0) for x in kept])
        columns = as_columns(kept)
        for i in range(LANES // block):
            for m in range(mass_count):
                for c in range(2):
                    at = i * block + m * rows + c * cap
                    outgoing[tile * (LANES // block) + i, c, m * cap : (m + 1) * cap, :] = columns[
                        at : at + cap
                    ]
        return carry

    lax.fori_loop(0, total // LANES, best, 0)

    list_rows = mass_count * cap

    def list_copy(k):
        target = shard_peer(k)
        return pltpu.make_async_remote_copy(
            src_ref=outgoing.at[target[1] // 2, lax.rem(target[1], 2)],
            dst_ref=lists.at[pl.ds(pl.multiple_of(shard * list_rows, list_rows), list_rows)],
            send_sem=list_send.at[k],
            recv_sem=list_recv.at[k],
            device_id=target,
            device_id_type=MESH,
        )

    def list_arrival(k):
        source = shard_peer(shard_count - k)
        return pltpu.make_async_remote_copy(
            src_ref=outgoing.at[0, 0],
            dst_ref=lists.at[pl.ds(pl.multiple_of(source[1] * list_rows, list_rows), list_rows)],
            send_sem=list_send.at[k],
            recv_sem=list_recv.at[k],
            device_id=source,
            device_id_type=MESH,
        )

    for k in range(1, shard_count):
        list_copy(k).start()
    lists[pl.ds(pl.multiple_of(shard * list_rows, list_rows), list_rows), :] = outgoing[
        place, core
    ]
    for k in range(1, shard_count):
        list_arrival(k).wait_recv()

    kept = None
    for tile in range(shard_count * list_rows // LANES):
        upright = lists[tile * LANES : (tile + 1) * LANES, :].T
        fresh = [jnp.broadcast_to(upright[i : i + 1, :], (8, LANES)) for i in range(TOP_K)]
        kept = fresh if kept is None else merge(kept, fresh)
    turn = list_rows
    while turn < LANES:
        kept = merge(kept, [pltpu.roll(x, turn, 1) for x in kept])
        turn *= 2
    merged[...] = as_columns(kept)[:list_rows]

    def group_rows(m):
        return pl.ds(pl.multiple_of(m * cap, cap), cap)

    def home_copy(k):
        target = mass_peer(k)
        return pltpu.make_async_remote_copy(
            src_ref=merged.at[group_rows(target[0])],
            dst_ref=homes.at[group_rows(mass)],
            send_sem=home_send.at[k],
            recv_sem=home_recv.at[k],
            device_id=target,
            device_id_type=MESH,
        )

    def home_arrival(k):
        source = mass_peer(mass_count - k)
        return pltpu.make_async_remote_copy(
            src_ref=merged.at[pl.ds(0, cap)],
            dst_ref=homes.at[group_rows(source[0])],
            send_sem=home_send.at[k],
            recv_sem=home_recv.at[k],
            device_id=source,
            device_id_type=MESH,
        )

    for k in range(1, mass_count):
        home_copy(k).start()
    homes[group_rows(mass), :] = merged[group_rows(mass), :]
    for k in range(1, mass_count):
        home_arrival(k).wait_recv()
    chosen = jnp.dot(
        owns[:, :list_rows],
        homes[...],
        preferred_element_type=F32,
        precision=lax.Precision.HIGHEST,
    )
    out_ref[...] = chosen

    swap.wait_send()
    swap_hot.wait_send()

    def finish(origin, carry):
        for way, there in (
            (0, (place + 1 < places) & (origin <= place)),
            (1, (place > 0) & (origin >= place)),
        ):

            @pl.when(there)
            def _():
                hot_copy(origin, way).wait_send()
                for part in range(turned):
                    line_copy(origin, part, way).wait_send()
                slots_copy(origin, turned, way).wait_send()

        for part in range(turned):
            for hop in range(1, mass_count):
                layer_copy(origin, part, hop).wait_send()

        @pl.when(origin == place)
        def _():
            for hop in range(1, mass_count):
                layer_copy(origin, turned, hop).wait_send()

        for part in range(parts):
            pair_copy(origin, part, core).wait_send()
        return carry

    lax.fori_loop(0, places, finish, 0)
    for k in range(1, shard_count):
        list_copy(k).wait_send()
    for k in range(1, mass_count):
        home_copy(k).wait_send()


def per_device(mass_count, shard_count, queries, library, routes, offsets):
    rows, bins = queries.shape
    half = bins // 2
    places = shard_count // 2
    cap = rows // 2
    block = mass_count * rows
    total = places * block
    width = half // PARTS
    anywhere = pl.BlockSpec(memory_space=pl.ANY)
    dma = pltpu.SemaphoreType.DMA
    best = pl.pallas_call(
        functools.partial(search_kernel, mass_count, shard_count),
        out_shape=jax.ShapeDtypeStruct((rows, LANES), F32),
        in_specs=[anywhere] * 4,
        out_specs=pl.BlockSpec(memory_space=pltpu.VMEM),
        scratch_shapes=[
            pltpu.VMEM((rows, bins), BF16),
            pltpu.VMEM((1, rows), jnp.int32),
            pltpu.VMEM((1, rows), jnp.int32),
            pltpu.VMEM((2, PARTS, rows, width), BF16),
            pltpu.VMEM((rows, LANES), BF16),
            pltpu.VMEM((rows, LANES), F32),
            pltpu.VMEM(library.shape, BF16),
            pltpu.VMEM((places, PARTS, 2 * rows, width), BF16),
            pltpu.VMEM((places, 2 * rows, LANES), BF16),
            pltpu.VMEM((places, PARTS, block, width), BF16),
            pltpu.VMEM((2, PARTS, total, width), BF16),
            pltpu.VMEM((library.shape[0], total), F32),
            pltpu.VMEM((places, 2, mass_count * cap, LANES), F32),
            pltpu.VMEM((shard_count * mass_count * cap, LANES), F32),
            pltpu.VMEM((mass_count * cap, LANES), F32),
            pltpu.VMEM((mass_count * cap, LANES), F32),
            dma,
            dma((3,)),
            dma((5,)),
            dma((2, places)),
            dma((places,)),
            dma((2, places * PARTS)),
            dma((places * PARTS,)),
            dma((places * PARTS, mass_count)),
            dma((places * PARTS, mass_count)),
            dma((places * PARTS,)),
            dma((places * PARTS,)),
            dma((shard_count,)),
            dma((shard_count,)),
            dma((mass_count,)),
            dma((mass_count,)),
        ],
        compiler_params=pltpu.CompilerParams(
            collective_id=0, has_side_effects=True, vmem_limit_bytes=56 * 2**20
        ),
    )(queries, offsets.reshape(1, rows), routes.reshape(1, rows), library)
    return best[:, :TOP_K]


def solution(mesh):
    placed = (
        P(("mass", "shard"), None),
        P(("mass", "shard"), None),
        P(("mass", "shard"), None),
        P(("mass", "shard")),
    )
    return jax.shard_map(
        functools.partial(per_device, mesh.shape["mass"], mesh.shape["shard"]),
        mesh=mesh,
        in_specs=placed,
        out_specs=P(("mass", "shard"), None),
        check_vma=False,
    )
```

```python
import functools

import jax
import jax.numpy as jnp
from jax import lax
from jax.experimental import pallas as pl
from jax.experimental.pallas import tpu as pltpu
from jax.sharding import PartitionSpec as P

MESH = pl.DeviceIdType.MESH
MAX_SHIFT = 2048
TOP_K = 16
LANES = 128
PARTS = 4
F32 = jnp.float32
BF16 = jnp.bfloat16


def comparators(count):
    pairs = []
    p = 1
    while p < count:
        k = p
        while k >= 1:
            for j in range(k % p, count - k, 2 * k):
                for i in range(min(k, count - j - k)):
                    if (i + j) // (2 * p) == (i + j + k) // (2 * p):
                        pairs.append((i + j, i + j + k))
            k //= 2
        p *= 2
    return pairs


def exchange(values, pairs):
    values = list(values)
    for i, j in pairs:
        a, b = values[i], values[j]
        values[i], values[j] = jnp.maximum(a, b), jnp.minimum(a, b)
    return values


SORT = comparators(TOP_K)
BITONIC = [
    (i, i + d) for d in (8, 4, 2, 1) for i in range(TOP_K) if i & d == 0
]


def merge(first, second):
    kept = [jnp.maximum(first[i], second[TOP_K - 1 - i]) for i in range(TOP_K)]
    return exchange(kept, BITONIC)


def spectra_parts(core, queries_ref, offsets_ref, routes_ref, halves, hots, owns):
    rows, bins = queries_ref.shape
    half = bins // 2
    parts, width = halves.shape[1], halves.shape[3]
    capacity = rows // 2
    down = lax.broadcasted_iota(jnp.int32, (rows, rows), 0)
    right = lax.broadcasted_iota(jnp.int32, (rows, rows), 1)

    def as_column(row):
        spread = jnp.broadcast_to(row.astype(F32), (rows, rows))
        return jnp.sum(jnp.where(down == right, spread, 0.0), axis=1, keepdims=True).astype(
            jnp.int32
        )

    plain = queries_ref[...].astype(F32)
    margin = jnp.zeros((rows, MAX_SHIFT), F32)
    current = jnp.concatenate([margin, plain, margin], axis=1)
    start = MAX_SHIFT - as_column(offsets_ref[...])
    step = 2 * MAX_SHIFT
    current = jnp.where(
        (start & step) != 0,
        jnp.concatenate([current[:, step:], jnp.zeros((rows, step), F32)], axis=1),
        current,
    )
    step //= 2
    while step >= LANES:
        wide = bins + step
        current = jnp.where(
            (start & step) != 0, current[:, step : step + wide], current[:, :wide]
        )
        step //= 2
    wide = bins + LANES
    while step >= 1:
        moved = pltpu.roll(current, wide - step, 1)
        current = jnp.where((start & step) != 0, moved, current)
        step //= 2
    combined = plain + current[:, :bins]
    scale = lax.rsqrt(jnp.sum(combined * combined, axis=1, keepdims=True) * (1.0 / bins) + 1e-06)
    spectra = (combined * scale).astype(BF16)
    group = as_column(routes_ref[...])
    earlier = (group == routes_ref[...]) & (down > right)
    rank = jnp.sum(jnp.where(earlier, 1.0, 0.0), axis=1, keepdims=True).astype(jnp.int32)
    lane = lax.broadcasted_iota(jnp.int32, (rows, LANES), 1)
    slot = group * (2 * capacity) + core * capacity + rank
    hots[...] = jnp.where(lane == slot, 1.0, 0.0).astype(BF16)
    owns[...] = jnp.where(lane == group * capacity + rank, 1.0, 0.0)
    for side in range(2):
        for part in range(parts):
            at = side * half + part * width
            halves[side, part] = spectra[:, at : at + width]


def search_kernel(
    mass_count,
    shard_count,
    queries_ref,
    offsets_ref,
    routes_ref,
    library_ref,
    out_ref,
    plain,
    shifts,
    groups,
    halves,
    hots,
    owns,
    lib,
    held,
    held_hots,
    packed,
    slots,
    scores,
    outgoing,
    lists,
    merged,
    homes,
    lib_sem,
    load_sem,
    start_sem,
    hot_send,
    hot_recv,
    line_send,
    line_recv,
    layer_send,
    layer_recv,
    pair_send,
    pair_recv,
    list_send,
    list_recv,
    home_send,
    home_recv,
):
    places = shard_count // 2
    parts, rows, width = halves.shape[1:]
    half = parts * width
    cap = rows // 2
    block = mass_count * rows
    total = places * block
    mass = lax.axis_index("mass")
    shard = lax.axis_index("shard")
    place = shard // 2
    core = lax.rem(shard, 2)
    sibling = (mass, shard + 1 - 2 * core)

    loads = [
        pltpu.make_async_copy(source, target, load_sem.at[i])
        for i, (source, target) in enumerate(
            [(queries_ref, plain), (offsets_ref, shifts), (routes_ref, groups)]
        )
    ]
    for load in loads:
        load.start()
    lib_copy = pltpu.make_async_copy(library_ref, lib, lib_sem)
    barrier = pltpu.get_barrier_semaphore()

    def greet(device):
        pl.semaphore_signal(barrier, inc=1, device_id=device, device_id_type=MESH)

    def mass_peer(k):
        return (lax.rem(mass + k, mass_count), shard)

    def shard_peer(k):
        return (mass, lax.rem(shard + k, shard_count))

    for k in range(1, mass_count):
        greet(mass_peer(k))
    for k in range(1, shard_count):
        greet(shard_peer(k))
    for load in loads:
        load.wait()
    lib_copy.start()
    spectra_parts(core, plain, shifts, groups, halves, hots, owns)
    pl.semaphore_wait(barrier, mass_count + shard_count - 2)

    mine = pl.ds(pl.multiple_of(core * rows, rows), rows)
    swap = pltpu.make_async_remote_copy(
        src_ref=halves.at[1 - core],
        dst_ref=held.at[place, :, mine, :],
        send_sem=start_sem.at[0],
        recv_sem=start_sem.at[1],
        device_id=sibling,
        device_id_type=MESH,
    )
    swap.start()
    swap_hot = pltpu.make_async_remote_copy(
        src_ref=hots,
        dst_ref=held_hots.at[place, mine, :],
        send_sem=start_sem.at[3],
        recv_sem=start_sem.at[4],
        device_id=sibling,
        device_id_type=MESH,
    )
    swap_hot.start()
    keep = pltpu.make_async_copy(halves.at[core], held.at[place, :, mine, :], start_sem.at[2])
    keep.start()
    held_hots[place, mine, :] = hots[...]
    keep.wait()
    swap_hot.wait_recv()
    swap.wait_recv()

    def hot_copy(origin, way):
        return pltpu.make_async_remote_copy(
            src_ref=held_hots.at[origin],
            dst_ref=held_hots.at[origin],
            send_sem=hot_send.at[way, origin],
            recv_sem=hot_recv.at[origin],
            device_id=(mass, shard + (2 if way == 0 else -2)),
            device_id_type=MESH,
        )

    def line_copy(origin, part, way):
        return pltpu.make_async_remote_copy(
            src_ref=held.at[origin, part],
            dst_ref=held.at[origin, part],
            send_sem=line_send.at[way, origin * parts + part],
            recv_sem=line_recv.at[origin * parts + part],
            device_id=(mass, shard + (2 if way == 0 else -2)),
            device_id_type=MESH,
        )

    def layer_rows(origin, source):
        return pl.ds(pl.multiple_of(origin * block + source * rows, rows), rows)

    def layer_copy(origin, part, hop):
        target = lax.rem(mass + hop, mass_count)
        return pltpu.make_async_remote_copy(
            src_ref=packed.at[origin, part, layer_rows(0, target)],
            dst_ref=slots.at[core, part, layer_rows(origin, mass)],
            send_sem=layer_send.at[origin * parts + part, hop],
            recv_sem=layer_recv.at[origin * parts + part, hop],
            device_id=(target, shard),
            device_id_type=MESH,
        )

    def layer_arrival(origin, part, hop):
        source = lax.rem(mass + mass_count - hop, mass_count)
        return pltpu.make_async_remote_copy(
            src_ref=packed.at[origin, part, pl.ds(0, rows)],
            dst_ref=slots.at[core, part, layer_rows(origin, source)],
            send_sem=layer_send.at[origin * parts + part, hop],
            recv_sem=layer_recv.at[origin * parts + part, hop],
            device_id=(source, shard),
            device_id_type=MESH,
        )

    def pair_copy(origin, part, side):
        span = slots.at[side, part, pl.ds(pl.multiple_of(origin * block, block), block)]
        return pltpu.make_async_remote_copy(
            src_ref=span,
            dst_ref=span,
            send_sem=pair_send.at[origin * parts + part],
            recv_sem=pair_recv.at[origin * parts + part],
            device_id=sibling,
            device_id_type=MESH,
        )

    tile = width

    def dispatch(origin, part):
        hot = held_hots[origin].astype(F32).T[:block].astype(BF16)

        def pack(j, carry):
            span = pl.ds(pl.multiple_of(j * tile, tile), tile)
            packed[origin, part, :, span] = jnp.dot(
                hot, held[origin, part, :, span], preferred_element_type=F32
            ).astype(BF16)
            return carry

        lax.fori_loop(0, width // tile, pack, 0)
        for hop in range(1, mass_count):
            layer_copy(origin, part, hop).start()
        slots[core, part, layer_rows(origin, mass), :] = packed[
            origin, part, layer_rows(0, mass), :
        ]

    def leave(part):
        for way, there in ((0, place + 1 < places), (1, place > 0)):

            @pl.when(there)
            def _():
                if part == 0:
                    hot_copy(place, way).start()
                line_copy(place, part, way).start()

    def take(origin, part, way, there):
        if part == 0:
            hot_copy(origin, way).wait_recv()
        line_copy(origin, part, way).wait_recv()

        @pl.when(there)
        def _():
            if part == 0:
                hot_copy(origin, way).start()
            line_copy(origin, part, way).start()

        dispatch(origin, part)

    def hop(part, t):
        below, above = place - 1 - t, place + 1 + t

        @pl.when(below >= 0)
        def _():
            take(below, part, 0, place + 1 < places)

        @pl.when(above < places)
        def _():
            take(above, part, 1, place > 0)

    def slots_copy(origin, part, way):
        span = slots.at[core, part, pl.ds(pl.multiple_of(origin * block, block), block)]
        return pltpu.make_async_remote_copy(
            src_ref=span,
            dst_ref=span,
            send_sem=line_send.at[way, origin * parts + part],
            recv_sem=line_recv.at[origin * parts + part],
            device_id=(mass, shard + (2 if way == 0 else -2)),
            device_id_type=MESH,
        )

    def leave_slots(part):
        for hop in range(1, mass_count):
            layer_arrival(place, part, hop).wait_recv()
        for way, there in ((0, place + 1 < places), (1, place > 0)):

            @pl.when(there)
            def _():
                slots_copy(place, part, way).start()

        pair_copy(place, part, core).start()

    def take_slots(origin, part, way, there):
        slots_copy(origin, part, way).wait_recv()

        @pl.when(there)
        def _():
            slots_copy(origin, part, way).start()

        pair_copy(origin, part, core).start()

    def hop_slots(part, t):
        below, above = place - 1 - t, place + 1 + t

        @pl.when(below >= 0)
        def _():
            take_slots(below, part, 0, place + 1 < places)

        @pl.when(above < places)
        def _():
            take_slots(above, part, 1, place > 0)

    def hand_over(part):
        def one(origin):
            for hop in range(1, mass_count):
                layer_arrival(origin, part, hop).wait_recv()
            pair_copy(origin, part, core).start()

        one(place)

        def advance(t, carry):
            for origin in (place - 1 - t, place + 1 + t):

                @pl.when((origin >= 0) & (origin < places))
                def _():
                    one(origin)

            return carry

        lax.fori_loop(0, places - 1, advance, 0)

    lib_rows = lib.shape[0]
    tall, wide = lib_rows, min(256, total)

    def multiply(part):
        lax.fori_loop(
            0, places, lambda o, x: (pair_copy(o, part, 1 - core).wait_recv(), x)[1], 0
        )

        def score(k, carry):
            i, j = k // (total // wide), lax.rem(k, total // wide)
            down = pl.ds(pl.multiple_of(i * tall, tall), tall)
            across = pl.ds(pl.multiple_of(j * wide, wide), wide)
            sums = None if part == 0 else scores[down, across]
            for side in range(2):
                at = side * half + part * width
                term = lax.dot_general(
                    lib[down, at : at + width],
                    slots[side, part, across, :],
                    (((1,), (1,)), ((), ())),
                    preferred_element_type=F32,
                )
                sums = term if sums is None else sums + term
            scores[down, across] = sums
            return carry

        lax.fori_loop(0, (lib_rows // tall) * (total // wide), score, 0)

    for part in range(2):
        leave(part)

    turned = parts - 1
    dispatch(place, turned)

    def fill(step, carry):
        for part in range(2, turned):

            @pl.when(step == part - 2)
            def _():
                leave(part)

        for part in range(turned):

            @pl.when((step > part) & (step - part < places))
            def _():
                hop(part, step - 1 - part)

            @pl.when(step == part)
            def _():
                dispatch(place, part)

        @pl.when(step == 1)
        def _():
            leave_slots(turned)

        @pl.when((step > 1) & (step - 2 < places - 1))
        def _():
            hop_slots(turned, step - 2)

        return carry

    steady = max(places, parts)
    lax.fori_loop(0, steady, fill, 0)
    for step in range(steady, steady + turned + 1):
        for part in range(turned):
            if 0 <= step - 1 - part < places - 1:
                hop(part, step - 1 - part)
        if step - 2 < places - 1:
            hop_slots(turned, step - 2)
        if step - steady < turned:
            hand_over(step - steady)
        if step == steady + 1:
            lib_copy.wait()
        if step == steady + turned:
            multiply(turned)
        if step > steady:
            multiply(step - steady - 1)

    sub = lax.broadcasted_iota(jnp.int32, (8, LANES), 0)

    def as_columns(values):
        upper, lower = values[0], values[8]
        for i in range(1, 8):
            upper = jnp.where(sub == i, values[i], upper)
            lower = jnp.where(sub == i, values[8 + i], lower)
        rest = jnp.zeros((LANES - TOP_K, LANES), F32)
        return jnp.concatenate([upper, lower, rest], axis=0).T

    stride = lib_rows // TOP_K

    def best(tile, carry):
        across = pl.ds(pl.multiple_of(tile * LANES, LANES), LANES)

        def more(r, kept):
            fresh = [
                scores[pl.ds(pl.multiple_of(i * stride + r * 8, 8), 8), across]
                for i in range(TOP_K)
            ]
            return tuple(merge(kept, exchange(fresh, SORT)))

        kept = tuple(jnp.full((8, LANES), -jnp.inf, F32) for _ in range(TOP_K))
        kept = lax.fori_loop(0, stride // 8, more, kept)
        for d in (4, 2, 1):
            kept = merge(kept, [pltpu.roll(x, d, 0) for x in kept])
        columns = as_columns(kept)
        for i in range(LANES // block):
            for m in range(mass_count):
                for c in range(2):
                    at = i * block + m * rows + c * cap
                    outgoing[tile * (LANES // block) + i, c, m * cap : (m + 1) * cap, :] = columns[
                        at : at + cap
                    ]
        return carry

    lax.fori_loop(0, total // LANES, best, 0)

    list_rows = mass_count * cap

    def list_copy(k):
        target = shard_peer(k)
        return pltpu.make_async_remote_copy(
            src_ref=outgoing.at[target[1] // 2, lax.rem(target[1], 2)],
            dst_ref=lists.at[pl.ds(pl.multiple_of(shard * list_rows, list_rows), list_rows)],
            send_sem=list_send.at[k],
            recv_sem=list_recv.at[k],
            device_id=target,
            device_id_type=MESH,
        )

    def list_arrival(k):
        source = shard_peer(shard_count - k)
        return pltpu.make_async_remote_copy(
            src_ref=outgoing.at[0, 0],
            dst_ref=lists.at[pl.ds(pl.multiple_of(source[1] * list_rows, list_rows), list_rows)],
            send_sem=list_send.at[k],
            recv_sem=list_recv.at[k],
            device_id=source,
            device_id_type=MESH,
        )

    for k in range(1, shard_count):
        list_copy(k).start()
    lists[pl.ds(pl.multiple_of(shard * list_rows, list_rows), list_rows), :] = outgoing[
        place, core
    ]
    for k in range(1, shard_count):
        list_arrival(k).wait_recv()

    kept = None
    for tile in range(shard_count * list_rows // LANES):
        upright = lists[tile * LANES : (tile + 1) * LANES, :].T
        fresh = [jnp.broadcast_to(upright[i : i + 1, :], (8, LANES)) for i in range(TOP_K)]
        kept = fresh if kept is None else merge(kept, fresh)
    turn = list_rows
    while turn < LANES:
        kept = merge(kept, [pltpu.roll(x, turn, 1) for x in kept])
        turn *= 2
    merged[...] = as_columns(kept)[:list_rows]

    def group_rows(m):
        return pl.ds(pl.multiple_of(m * cap, cap), cap)

    def home_copy(k):
        target = mass_peer(k)
        return pltpu.make_async_remote_copy(
            src_ref=merged.at[group_rows(target[0])],
            dst_ref=homes.at[group_rows(mass)],
            send_sem=home_send.at[k],
            recv_sem=home_recv.at[k],
            device_id=target,
            device_id_type=MESH,
        )

    def home_arrival(k):
        source = mass_peer(mass_count - k)
        return pltpu.make_async_remote_copy(
            src_ref=merged.at[pl.ds(0, cap)],
            dst_ref=homes.at[group_rows(source[0])],
            send_sem=home_send.at[k],
            recv_sem=home_recv.at[k],
            device_id=source,
            device_id_type=MESH,
        )

    for k in range(1, mass_count):
        home_copy(k).start()
    homes[group_rows(mass), :] = merged[group_rows(mass), :]
    for k in range(1, mass_count):
        home_arrival(k).wait_recv()
    chosen = jnp.dot(
        owns[:, :list_rows],
        homes[...],
        preferred_element_type=F32,
        precision=lax.Precision.HIGHEST,
    )
    out_ref[...] = chosen

    swap.wait_send()
    swap_hot.wait_send()

    def finish(origin, carry):
        for way, there in (
            (0, (place + 1 < places) & (origin <= place)),
            (1, (place > 0) & (origin >= place)),
        ):

            @pl.when(there)
            def _():
                hot_copy(origin, way).wait_send()
                for part in range(turned):
                    line_copy(origin, part, way).wait_send()
                slots_copy(origin, turned, way).wait_send()

        for part in range(turned):
            for hop in range(1, mass_count):
                layer_copy(origin, part, hop).wait_send()

        @pl.when(origin == place)
        def _():
            for hop in range(1, mass_count):
                layer_copy(origin, turned, hop).wait_send()

        for part in range(parts):
            pair_copy(origin, part, core).wait_send()
        return carry

    lax.fori_loop(0, places, finish, 0)
    for k in range(1, shard_count):
        list_copy(k).wait_send()
    for k in range(1, mass_count):
        home_copy(k).wait_send()


def per_device(mass_count, shard_count, queries, library, routes, offsets):
    rows, bins = queries.shape
    half = bins // 2
    places = shard_count // 2
    cap = rows // 2
    block = mass_count * rows
    total = places * block
    width = half // PARTS
    anywhere = pl.BlockSpec(memory_space=pl.ANY)
    dma = pltpu.SemaphoreType.DMA
    best = pl.pallas_call(
        functools.partial(search_kernel, mass_count, shard_count),
        out_shape=jax.ShapeDtypeStruct((rows, LANES), F32),
        in_specs=[anywhere] * 4,
        out_specs=pl.BlockSpec(memory_space=pltpu.VMEM),
        scratch_shapes=[
            pltpu.VMEM((rows, bins), BF16),
            pltpu.VMEM((1, rows), jnp.int32),
            pltpu.VMEM((1, rows), jnp.int32),
            pltpu.VMEM((2, PARTS, rows, width), BF16),
            pltpu.VMEM((rows, LANES), BF16),
            pltpu.VMEM((rows, LANES), F32),
            pltpu.VMEM(library.shape, BF16),
            pltpu.VMEM((places, PARTS, 2 * rows, width), BF16),
            pltpu.VMEM((places, 2 * rows, LANES), BF16),
            pltpu.VMEM((places, PARTS, block, width), BF16),
            pltpu.VMEM((2, PARTS, total, width), BF16),
            pltpu.VMEM((library.shape[0], total), F32),
            pltpu.VMEM((places, 2, mass_count * cap, LANES), F32),
            pltpu.VMEM((shard_count * mass_count * cap, LANES), F32),
            pltpu.VMEM((mass_count * cap, LANES), F32),
            pltpu.VMEM((mass_count * cap, LANES), F32),
            dma,
            dma((3,)),
            dma((5,)),
            dma((2, places)),
            dma((places,)),
            dma((2, places * PARTS)),
            dma((places * PARTS,)),
            dma((places * PARTS, mass_count)),
            dma((places * PARTS, mass_count)),
            dma((places * PARTS,)),
            dma((places * PARTS,)),
            dma((shard_count,)),
            dma((shard_count,)),
            dma((mass_count,)),
            dma((mass_count,)),
        ],
        compiler_params=pltpu.CompilerParams(
            collective_id=0, has_side_effects=True, vmem_limit_bytes=56 * 2**20
        ),
    )(queries, offsets.reshape(1, rows), routes.reshape(1, rows), library)
    return best[:, :TOP_K]


def solution(mesh):
    placed = (
        P(("mass", "shard"), None),
        P(("mass", "shard"), None),
        P(("mass", "shard"), None),
        P(("mass", "shard")),
    )
    return jax.shard_map(
        functools.partial(per_device, mesh.shape["mass"], mesh.shape["shard"]),
        mesh=mesh,
        in_specs=placed,
        out_specs=P(("mass", "shard"), None),
        check_vma=False,
    )
```
